256 devices in a mesh: hid: 64 (over x, y_lo, z), mod: 4 (over y_hi, core).
Axes of the slice: x: 4, y: 4 (y_hi: 2, y_lo: 2; y = y_hi * 2 + y_lo), z: 8, core: 2. Of those that a mesh axis runs over, the one named last changes fastest.
Arguments:
- tokens: bfloat16 [1024, 8192], P('hid', 'mod'), may hold values from -6 to 6
- grad_output: bfloat16 [1024, 8192], P('hid', 'mod'), may hold values from -6 to 6
- gate_weight: bfloat16 [8192, 28672], P('mod', 'hid'), may hold values from -0.0625 to 0.0625
- up_weight: bfloat16 [8192, 28672], P('mod', 'hid'), may hold values from -0.0625 to 0.0625
- down_weight: bfloat16 [28672, 8192], P('hid', 'mod'), may hold values from -0.03125 to 0.03125
Outputs:
- grad_tokens: bfloat16 [1024, 8192], P('hid', 'mod')
- grad_gate: bfloat16 [8192, 28672], P('mod', 'hid')
- grad_up: bfloat16 [8192, 28672], P('mod', 'hid')
- grad_down: bfloat16 [28672, 8192], P('hid', 'mod')
The draws below stay inside these ranges and needn't reach their ends.
All inputs are finite; a program needn't handle non-finite values.
Results may differ from the reference program's by a relative error of at most 0.0049.
Values may be sent and summed in bfloat16 or wider, within the bound.
A program may use at most 128 MiB of HBM per device.

```python
import jax
import jax.numpy as jnp
from jax import lax

D = 8192
FF = 28672
TOKENS = 1024


def shard_levels(stream_key, extent, cuts, smallest, largest):
    def one(dim, parts):
        steps = jax.random.uniform(jax.random.fold_in(jax.random.fold_in(stream_key, 6), dim), (parts,), jnp.float32, smallest / len(cuts), largest / len(cuts))
        return jnp.repeat(jnp.exp(steps), extent[dim] // parts).reshape((-1,) + (1,) * (len(extent) - dim - 1))

    loudness = one(*cuts[0])
    for cut in cuts[1:]:
        loudness = loudness * one(*cut)
    return loudness


def scatter_about(own_key, dims, spread, limit, cuts=(), dtype=jnp.bfloat16):
    gain = shard_levels(own_key, dims, cuts, -0.22, 0.18) if cuts else 1.0
    result = jax.random.normal(own_key, dims, jnp.float32) * spread * gain
    return jnp.minimum(jnp.maximum(result, -limit), limit).astype(dtype)


def setup_inputs(seed: int = 0) -> dict:
    arg_keys = jax.random.split(jax.random.key(seed), 6)
    tokens = scatter_about(arg_keys[0], (TOKENS, D), 1.0, 6.0, ((0, 64), (1, 4)))
    grad_output = scatter_about(arg_keys[1], (TOKENS, D), 1.0, 6.0, ((0, 64), (1, 4)))
    gate_weight = scatter_about(arg_keys[2], (D, FF), D ** -0.5, 0.0625, ((0, 4), (1, 64)))
    up_weight = scatter_about(arg_keys[3], (D, FF), D ** -0.5, 0.0625, ((0, 4), (1, 64)))
    down_weight = scatter_about(arg_keys[4], (FF, D), FF ** -0.5, 0.03125, ((0, 64), (1, 4)))
    return dict(tokens=tokens, grad_output=grad_output, gate_weight=gate_weight, up_weight=up_weight, down_weight=down_weight)


def swiglu_back(gate, up, grad_hidden):
    sigmoid_gate = jax.nn.sigmoid(gate)
    active = gate * sigmoid_gate
    hidden = (active * up).astype(jnp.bfloat16)
    up_back = (grad_hidden * active).astype(jnp.bfloat16)
    slope = sigmoid_gate * (1.0 + gate * (1.0 - sigmoid_gate))
    gate_back = (grad_hidden * up * slope).astype(jnp.bfloat16)
    return hidden, gate_back, up_back


def reference(tokens, grad_output, gate_weight, up_weight, down_weight):
    gate = jnp.dot(tokens, gate_weight, preferred_element_type=jnp.float32)
    up = jnp.dot(tokens, up_weight, preferred_element_type=jnp.float32)
    grad_hidden = lax.dot_general(grad_output, down_weight, (((1,), (1,)), ((), ())), preferred_element_type=jnp.float32)
    hidden, gate_back, up_back = swiglu_back(gate, up, grad_hidden)
    contract_rows = (((0,), (0,)), ((), ()))
    grad_down = lax.dot_general(hidden, grad_output, contract_rows, preferred_element_type=jnp.float32).astype(jnp.bfloat16)
    grad_gate = lax.dot_general(tokens, gate_back, contract_rows, preferred_element_type=jnp.float32).astype(jnp.bfloat16)
    grad_up = lax.dot_general(tokens, up_back, contract_rows, preferred_element_type=jnp.float32).astype(jnp.bfloat16)
    contract_cols = (((1,), (1,)), ((), ()))
    total = lax.dot_general(gate_back, gate_weight, contract_cols, preferred_element_type=jnp.float32)
    total = total + lax.dot_general(up_back, up_weight, contract_cols, preferred_element_type=jnp.float32)
    grad_tokens = total.astype(jnp.bfloat16)
    return grad_tokens, grad_gate, grad_up, grad_down
```

```python
import functools

import jax
import jax.numpy as jnp
from jax import lax
from jax.experimental import pallas as pl
from jax.experimental.pallas import tpu as pltpu
from jax.sharding import PartitionSpec as P

MESH = pl.DeviceIdType.MESH
BF = jnp.bfloat16
F32 = jnp.float32
NT = (((1,), (1,)), ((), ()))

NX, NZ = 4, 8
SH = 16
PAIR = 2 * SH
CHUNK = NX * PAIR
TILES = 8

ORDER = (
    ('own',), ('y',), ('x0', 'T', 0), ('x0', 'T', 1), ('z', 1, 'T0'), ('z', 2, 'T0'), ('z', 1, 'C'), ('z', 2, 'C'),
    ('x0', 'C', 0), ('x0', 'C', 1), ('x0b', 'T'), ('z', 1, 'T1'), ('z', 2, 'T1'), ('x', 1, 0), ('x', 1, 1),
    ('z', 1, 'T2'), ('z', 2, 'T2'), ('x', 2, 0), ('x', 2, 1), ('z', 3, 'T0'), ('z', 4, 'T0'), ('x0b', 'C'), ('F', 0),
    ('xb', 1), ('z', 3, 'C'), ('z', 4, 'C'), ('xb', 2), ('G', 0), ('z', 1, 'T3'), ('z', 2, 'T3'), ('F', 1),
    ('x', 3, 0), ('x', 3, 1), ('F', 2), ('z', 3, 'T1'), ('z', 4, 'T1'), ('G', 1), ('H', 0), ('x', 4, 0), ('x', 4, 1),
    ('G', 2), ('z', 3, 'T2'), ('z', 4, 'T2'), ('xb', 3), ('xb', 4), ('z', 5, 'T0'), ('z', 6, 'T0'), ('H', 1),
    ('z', 5, 'C'), ('z', 6, 'C'), ('I', 0), ('J', 0), ('z', 3, 'T3'), ('z', 4, 'T3'), ('F', 3), ('x', 5, 0),
    ('x', 5, 1), ('H', 2), ('z', 5, 'T1'), ('z', 6, 'T1'), ('F', 4), ('x', 6, 0), ('x', 6, 1), ('I', 1), ('G', 3),
    ('z', 5, 'T2'), ('z', 6, 'T2'), ('K', 0), ('I', 2), ('G', 4), ('z', 7, 'T0'), ('xb', 5), ('J', 1), ('z', 7, 'C'),
    ('xb', 6), ('J', 2), ('H', 3), ('z', 5, 'T3'), ('z', 6, 'T3'), ('L', 0), ('F', 5), ('z', 7, 'T1'), ('K', 1),
    ('F', 6), ('z', 7, 'T2'), ('M', 0), ('H', 4), ('z', 7, 'T3'), ('x', 7, 0), ('x', 7, 1), ('G', 5), ('I', 3),
    ('K', 2), ('G', 6), ('J', 3), ('L', 1), ('I', 4), ('xb', 7), ('F', 7), ('J', 4), ('M', 1), ('L', 2), ('H', 5),
    ('G', 7), ('K', 3), ('K', 4), ('M', 2), ('H', 6), ('I', 5), ('L', 3), ('J', 5), ('L', 4), ('M', 3), ('H', 7),
    ('K', 5), ('M', 4), ('I', 6), ('J', 6), ('I', 7), ('L', 5), ('J', 7), ('K', 6), ('ht',), ('M', 5), ('W', 0),
    ('W', 1), ('K', 7), ('W', 2), ('L', 6), ('W', 3), ('W', 4), ('M', 6), ('L', 7), ('W', 5), ('W', 6), ('M', 7),
    ('W', 7), ('N',),
)


def distance(k):
    return (k + 1) // 2


class Step:
    def __init__(self, refs):
        (self.tok_in, self.cot_in, self.wg_in, self.wu_in, self.wd_in,
         self.out, self.og, self.ou, self.od,
         self.tok, self.cot, self.wg, self.wu, self.wd, self.part, self.s1, self.s2, self.back,
         self.tot, self.b1, self.b2, self.r1, self.r2, self.by, self.ry, self.bz, self.rz,
         self.vg, self.vu, self.vd, self.ht, self.send_sem, self.recv_sem, self.local_sem) = refs
        hid, mod = lax.axis_index("hid"), lax.axis_index("mod")
        self.x, self.yl, self.z = hid // 16, (hid // 8) % 2, hid % 8
        self.yh, self.c = mod // 2, mod % 2
        self.ids = {}
        self.sent = []
        self.n_local = 0
        self.local = []
        half = self.tok.shape[1] // 2
        self.half = (pl.ds(0, half), pl.ds(half, half))

    def dev(self, dx=0, dz=0, yl=None, yh=None, c=None):
        x = lax.rem(self.x + (dx + NX), NX)
        z = lax.rem(self.z + (dz + NZ), NZ)
        yl = self.yl if yl is None else yl
        yh = self.yh if yh is None else yh
        c = self.c if c is None else c
        return (x * 16 + yl * 8 + z, yh * 2 + c)

    def zchunk(self, k):
        d = distance(k) if k % 2 == 0 else -distance(k)
        return lax.rem(self.z + (d + NZ), NZ)

    def xblock(self, dx):
        return lax.rem(self.x + (dx + NX), NX)

    def rows(self, k, dx=None, y=None):
        base = self.zchunk(k) * CHUNK
        if dx is None:
            return pl.ds(pl.multiple_of(base, CHUNK), CHUNK)
        base = base + self.xblock(dx) * PAIR
        if y is None:
            return pl.ds(pl.multiple_of(base, PAIR), PAIR)
        return pl.ds(pl.multiple_of(base + y * SH, SH), SH)

    def quarter(self, k, c, yh):
        return pl.ds(pl.multiple_of(self.zchunk(k) * CHUNK + c * 64 + yh * 32, 32), 32)

    def sem(self, key):
        return self.ids.setdefault(key, len(self.ids))

    def send(self, key, src, dst, dev):
        i = self.sem(key)
        cp = pltpu.make_async_remote_copy(src_ref=src, dst_ref=dst, send_sem=self.send_sem.at[i],
                                          recv_sem=self.recv_sem.at[i], device_id=dev, device_id_type=MESH)
        cp.start()
        self.sent.append(cp)

    def wait(self, key, dst, dev):
        i = self.sem(key)
        pltpu.make_async_remote_copy(src_ref=dst, dst_ref=dst, send_sem=self.send_sem.at[i],
                                     recv_sem=self.recv_sem.at[i], device_id=dev, device_id_type=MESH).wait_recv()

    def fetch(self, src, dst):
        cp = pltpu.make_async_copy(src, dst, self.local_sem.at[self.n_local])
        self.n_local += 1
        cp.start()
        return cp

    def xd(self, q):
        return self.dev(dx=1 if q == 0 else -1)

    def zd(self, q):
        return self.dev(dz=1 if q == 0 else -1)

    def arr(self, a):
        return self.tok if a == "T" else self.cot

    def begin(self):
        own = self.rows(0, 0, self.yl)
        first = (self.fetch(self.tok_in, self.tok.at[own]), self.fetch(self.cot_in, self.cot.at[own]))
        self.weights = (self.fetch(self.wg_in, self.wg), self.fetch(self.wu_in, self.wu), self.fetch(self.wd_in, self.wd))
        bar = pltpu.get_barrier_semaphore()
        peers = [self.xd(0), self.xd(1), self.dev(yl=1 - self.yl), self.dev(yh=1 - self.yh), self.dev(c=1 - self.c)]
        peers += [self.dev(dz=d) for d in (1, -1, 2, -2, 3, -3, 4)]
        for p in peers:
            pl.semaphore_signal(bar, inc=1, device_id=p, device_id_type=MESH)
        pl.semaphore_wait(bar, len(peers))
        for cp in first:
            cp.wait()

    def plane(self, a, y, part):
        r = self.arr(a).at[self.rows(0, 0, y)]
        for q in (0, 1):
            self.send(("x0", a, q, part), r, r, self.xd(q))
        for q in (0, 1):
            self.send(("z", 1 + q, a + "o", part), r, r, self.zd(q))

    def own(self):
        for a in "TC":
            r = self.arr(a).at[self.rows(0, 0, self.yl)]
            self.send(("y", a), r, r, self.dev(yl=1 - self.yl))
        for a in "TC":
            self.plane(a, self.yl, 0)

    def y(self):
        for a in "TC":
            self.wait(("y", a), self.arr(a).at[self.rows(0, 0, 1 - self.yl)], self.dev(yl=1 - self.yl))
            self.plane(a, 1 - self.yl, 1)

    def x0(self, a, q):
        dx = -1 if q == 0 else 1
        for part, y in ((0, self.yl), (1, 1 - self.yl)):
            self.wait(("x0", a, q, part), self.arr(a).at[self.rows(0, dx, y)], self.xd(1 - q))
        r = self.arr(a).at[self.rows(0, dx)]
        h = self.arr(a).at[self.rows(0, dx), self.half[q]]
        self.send(("x0b", a, q), h, h, self.xd(q))
        if a == "T":
            for p in (0, 1):
                self.send(("z", 1 + p, "T%d" % (1 + q), 0), r, r, self.zd(p))

    def x0b(self, a):
        for q in (0, 1):
            self.wait(("x0b", a, q), self.arr(a).at[self.rows(0, 2), self.half[q]], self.xd(1 - q))
        if a == "T":
            r = self.tok.at[self.rows(0, 2)]
            for p in (0, 1):
                self.send(("z", 1 + p, "T3", 0), r, r, self.zd(p))

    def zin(self, k, p):
        d = 0 if k % 2 else 1
        a = self.arr(p[0])
        dx = {"C": 0, "T0": 0, "T1": -1, "T2": 1, "T3": 2}[p]
        r = a.at[self.rows(k, dx)]
        if k == 7:
            for q in (0, 1):
                self.wait(("z", 7, p, q), a.at[self.rows(k, dx), self.half[q]], self.zd(1 - q))
        elif k <= 2 and dx == 0:
            for part, y in ((0, self.yl), (1, 1 - self.yl)):
                self.wait(("z", k, p[0] + "o", part), a.at[self.rows(k, dx, y)], self.zd(1 - d))
        else:
            self.wait(("z", k, p, 0), r, self.zd(1 - d))
        if k < 5:
            self.send(("z", k + 2, p, 0), r, r, self.zd(d))
        elif k < 7:
            h = a.at[self.rows(k, dx), self.half[d]]
            self.send(("z", 7, p, d), h, h, self.zd(d))
        if p == "C":
            for q in (0, 1):
                self.send(("x", k, q), r, r, self.xd(q))

    def xin(self, k, q):
        dx = -1 if q == 0 else 1
        self.wait(("x", k, q), self.cot.at[self.rows(k, dx)], self.xd(1 - q))
        h = self.cot.at[self.rows(k, dx), self.half[q]]
        self.send(("xb", k, q), h, h, self.xd(q))

    def xb(self, k):
        for q in (0, 1):
            self.wait(("xb", k, q), self.cot.at[self.rows(k, 2), self.half[q]], self.xd(1 - q))

    def F(self, k):
        if k == 0:
            for cp in self.weights:
                cp.wait()
        r = self.rows(k)
        t = self.tok[r, :]
        self.part[k, 0] = jnp.dot(t, self.wg[...], preferred_element_type=F32)
        self.part[k, 1] = jnp.dot(t, self.wu[...], preferred_element_type=F32)
        self.part[k, 2] = lax.dot_general(self.cot[r, :], self.wd[...], NT, preferred_element_type=F32)
        other = pl.ds(pl.multiple_of((1 - self.c) * 64, 64), 64)
        self.send(("s1", k), self.part.at[k, :, other, :], self.s1.at[k], self.dev(c=1 - self.c))

    def G(self, k):
        self.wait(("s1", k), self.s1.at[k], self.dev(c=1 - self.c))
        there = pl.ds(pl.multiple_of((1 - self.yh) * 32, 32), 32)
        mine = pl.ds(pl.multiple_of(self.c * 64 + (1 - self.yh) * 32, 32), 32)
        self.part[k, :, mine, :] = self.part[k, :, mine, :] + self.s1[k, :, there, :]
        self.send(("s2", k), self.part.at[k, :, mine, :], self.s2.at[k], self.dev(yh=1 - self.yh))

    def H(self, k):
        self.wait(("s2", k), self.s2.at[k], self.dev(yh=1 - self.yh))
        here = pl.ds(pl.multiple_of(self.yh * 32, 32), 32)
        mine = pl.ds(pl.multiple_of(self.c * 64 + self.yh * 32, 32), 32)
        gate, up, grad = (self.part[k, i, mine, :] + self.s1[k, i, here, :] + self.s2[k, i] for i in range(3))
        s = jax.nn.sigmoid(gate)
        a = gate * s
        r = self.quarter(k, self.c, self.yh)
        self.back[0, r, :] = (a * up).astype(BF)
        self.back[1, r, :] = (grad * up * (s * (1.0 + gate * (1.0 - s)))).astype(BF)
        self.back[2, r, :] = (grad * a).astype(BF)
        b = self.back.at[:, r, :]
        self.send(("s3", k), b, b, self.dev(yh=1 - self.yh))
        self.send(("s4", k, 0), b, b, self.dev(c=1 - self.c))

    def I(self, k):
        b = self.back.at[:, self.quarter(k, self.c, 1 - self.yh), :]
        self.wait(("s3", k), b, self.dev(yh=1 - self.yh))
        self.send(("s4", k, 1), b, b, self.dev(c=1 - self.c))

    def J(self, k):
        for i, yh in ((0, self.yh), (1, 1 - self.yh)):
            self.wait(("s4", k, i), self.back.at[:, self.quarter(k, 1 - self.c, yh), :], self.dev(c=1 - self.c))
        r = self.rows(k)
        self.tot[k] = lax.dot_general(
            self.back[1, r, :], self.wg[...], NT, preferred_element_type=F32
        ) + lax.dot_general(self.back[2, r, :], self.wu[...], NT, preferred_element_type=F32)
        self.b1[k] = self.tot[k, self.block(2), :].astype(BF)
        for q in (0, 1):
            self.send(("r1", k, q), self.b1.at[k, :, self.half[q]], self.r1.at[k, q], self.xd(q))

    def block(self, dx):
        return pl.ds(pl.multiple_of(self.xblock(dx) * PAIR, PAIR), PAIR)

    def K(self, k):
        for q in (0, 1):
            self.wait(("r1", k, q), self.r1.at[k, q], self.xd(1 - q))
            b = self.block(1 if q == 0 else -1)
            self.b2[k, q, :, self.half[q]] = (self.tot[k, b, self.half[q]] + self.r1[k, q].astype(F32)).astype(BF)
            self.b2[k, q, :, self.half[1 - q]] = self.tot[k, b, self.half[1 - q]].astype(BF)
            self.send(("r2", k, q), self.b2.at[k, q], self.r2.at[k, q], self.xd(q))

    def L(self, k):
        for q in (0, 1):
            self.wait(("r2", k, q), self.r2.at[k, q], self.xd(1 - q))
        b = self.block(0)
        self.tot[k, b, :] = self.tot[k, b, :] + self.r2[k, 0].astype(F32) + self.r2[k, 1].astype(F32)
        self.by[k] = self.tot[k, self.yrows(1 - self.yl), :].astype(BF)
        self.send(("ry", k), self.by.at[k], self.ry.at[k], self.dev(yl=1 - self.yl))

    def yrows(self, y):
        return pl.ds(pl.multiple_of(self.xblock(0) * PAIR + y * SH, SH), SH)

    def M(self, k):
        self.wait(("ry", k), self.ry.at[k], self.dev(yl=1 - self.yl))
        s = self.tot[k, self.yrows(self.yl), :] + self.ry[k].astype(F32)
        if k == 0:
            self.tot[k, self.yrows(self.yl), :] = s
        else:
            self.bz[k] = s.astype(BF)
            d = distance(k) if k % 2 == 0 else -distance(k)
            self.send(("rz", k), self.bz.at[k], self.rz.at[k], self.dev(dz=d))

    def N(self):
        s = self.tot[0, self.yrows(self.yl), :]
        for k in range(1, 8):
            d = distance(k) if k % 2 == 0 else -distance(k)
            self.wait(("rz", k), self.rz.at[k], self.dev(dz=-d))
            s = s + self.rz[k].astype(F32)
        self.out[...] = s.astype(BF)

    def turn(self):
        self.ht[...] = self.back[0].T

    def W(self, j):
        n = self.tok.shape[1] // TILES
        cs = pl.ds(j * n, n)
        lt = self.tok[:, cs].T
        self.vg[cs, :] = jnp.dot(lt, self.back[1], preferred_element_type=F32).astype(BF)
        self.vu[cs, :] = jnp.dot(lt, self.back[2], preferred_element_type=F32).astype(BF)
        self.vd[:, cs] = jnp.dot(self.ht[...], self.cot[:, cs], preferred_element_type=F32).astype(BF)
        self.local.append(self.fetch(self.vg.at[cs, :], self.og.at[cs, :]))
        self.local.append(self.fetch(self.vu.at[cs, :], self.ou.at[cs, :]))
        self.local.append(self.fetch(self.vd.at[:, cs], self.od.at[:, cs]))

    def finish(self):
        for cp in self.sent:
            cp.wait_send()
        for cp in self.local:
            cp.wait()


NAMES = {"z": "zin", "x": "xin", "ht": "turn"}


def kernel(*refs):
    step = Step(refs)
    step.begin()
    for name, *args in ORDER:
        getattr(step, NAMES.get(name, name))(*args)
    step.finish()


def shards(tokens, grad_output, gate_weight, up_weight, down_weight):
    d, f = gate_weight.shape
    n = NZ * CHUNK
    anywhere = pl.BlockSpec(memory_space=pl.ANY)
    vmem = pltpu.VMEM
    return pl.pallas_call(
        kernel,
        out_shape=(
            jax.ShapeDtypeStruct((SH, d), BF),
            jax.ShapeDtypeStruct((d, f), BF),
            jax.ShapeDtypeStruct((d, f), BF),
            jax.ShapeDtypeStruct((f, d), BF),
        ),
        in_specs=[anywhere] * 5,
        out_specs=(pl.BlockSpec(memory_space=vmem), anywhere, anywhere, anywhere),
        scratch_shapes=[
            vmem((n, d), BF), vmem((n, d), BF),
            vmem((d, f), BF), vmem((d, f), BF), vmem((f, d), BF),
            vmem((NZ, 3, CHUNK, f), F32), vmem((NZ, 3, 64, f), F32), vmem((NZ, 3, 32, f), F32),
            vmem((3, n, f), BF),
            vmem((NZ, CHUNK, d), F32),
            vmem((NZ, PAIR, d), BF), vmem((NZ, 2, PAIR, d), BF),
            vmem((NZ, 2, PAIR, d // 2), BF), vmem((NZ, 2, PAIR, d), BF),
            vmem((NZ, SH, d), BF), vmem((NZ, SH, d), BF), vmem((NZ, SH, d), BF), vmem((NZ, SH, d), BF),
            vmem((d, f), BF), vmem((d, f), BF), vmem((f, d), BF), vmem((f, n), BF),
            pltpu.SemaphoreType.DMA((200,)), pltpu.SemaphoreType.DMA((200,)), pltpu.SemaphoreType.DMA((5 + 3 * TILES,)),
        ],
        compiler_params=pltpu.CompilerParams(collective_id=0, has_side_effects=True, vmem_limit_bytes=62 << 20),
        cost_estimate=pl.CostEstimate(flops=16 * n * d * f, bytes_accessed=12 * d * f, transcendentals=n * f),
    )(tokens, grad_output, gate_weight, up_weight, down_weight)


def solution(mesh):
    placed = (P("hid", "mod"), P("hid", "mod"), P("mod", "hid"), P("mod", "hid"), P("hid", "mod"))
    return jax.shard_map(
        shards,
        mesh=mesh,
        in_specs=placed,
        out_specs=(P("hid", "mod"), P("mod", "hid"), P("mod", "hid"), P("hid", "mod")),
        check_vma=False,
    )
```

```python
import functools

import jax
import jax.numpy as jnp
from jax import lax
from jax.experimental import pallas as pl
from jax.experimental.pallas import tpu as pltpu
from jax.sharding import PartitionSpec as P

MESH = pl.DeviceIdType.MESH
BF = jnp.bfloat16
F32 = jnp.float32
NT = (((1,), (1,)), ((), ()))

NX, NZ = 4, 8
SH = 16
PAIR = 2 * SH
CHUNK = NX * PAIR
TILES = 8
ZC = ()
DIRECT = (7,)
FAR = (5, 6, 7)
COPIES = 2

ORDER = (
    ('own',), ('y',), ('x0', 'T', 0), ('x0', 'T', 1), ('z', 1, 'C'), ('z', 2, 'C'), ('z', 1, 'T0'), ('z', 2, 'T0'),
    ('x0', 'C', 0), ('x0', 'C', 1), ('x0b', 'T'), ('z', 1, 'T1'), ('z', 2, 'T1'), ('x', 1, 0), ('x', 1, 1),
    ('z', 1, 'T2'), ('z', 2, 'T2'), ('x', 2, 0), ('x', 2, 1), ('z', 3, 'C'), ('z', 4, 'C'), ('x0b', 'C'), ('F', 0),
    ('xb', 1), ('z', 3, 'T0'), ('z', 4, 'T0'), ('xb', 2), ('G', 0), ('z', 1, 'T3'), ('z', 2, 'T3'), ('F', 2),
    ('F', 1), ('x', 3, 0), ('z', 3, 'T1'), ('z', 4, 'T1'), ('x', 4, 0), ('G', 2), ('x', 4, 1), ('x', 3, 1), ('H', 0),
    ('G', 1), ('z', 3, 'T2'), ('z', 4, 'T2'), ('J', 0), ('xb', 4), ('xb', 3), ('z', 5, 'C'), ('z', 6, 'C'), ('H', 2),
    ('K', 0), ('z', 5, 'T0'), ('z', 6, 'T0'), ('J', 2), ('x', 5, 1), ('x', 5, 0), ('z', 3, 'T3'), ('F', 3),
    ('z', 4, 'T3'), ('H', 1), ('F', 4), ('G', 3), ('z', 5, 'T1'), ('z', 6, 'T1'), ('x', 6, 0), ('J', 1), ('L', 0),
    ('z', 5, 'T2'), ('z', 6, 'T2'), ('G', 4), ('x', 6, 1), ('K', 2), ('z', 7, 'C'), ('xb', 5), ('z', 7, 'T0'),
    ('H', 3), ('xb', 6), ('K', 1), ('z', 5, 'T3'), ('z', 6, 'T3'), ('F', 5), ('z', 7, 'T1'), ('M', 0), ('J', 3),
    ('z', 7, 'T2'), ('G', 5), ('F', 6), ('z', 7, 'T3'), ('x', 7, 1), ('x', 7, 0), ('L', 2), ('H', 4), ('G', 6),
    ('J', 4), ('L', 1), ('K', 3), ('H', 5), ('xb', 7), ('F', 7), ('J', 5), ('M', 2), ('G', 7), ('K', 4), ('L', 3),
    ('H', 6), ('M', 1), ('K', 5), ('J', 6), ('L', 4), ('H', 7), ('M', 3), ('L', 5), ('J', 7), ('M', 4), ('K', 6),
    ('ht',), ('W', 0), ('W', 1), ('W', 2), ('W', 3), ('W', 4), ('L', 7), ('W', 5), ('W', 6), ('L', 6), ('W', 7),
    ('N',),
)


def distance(k):
    return (k + 1) // 2


def offset(k):
    return distance(k) if k % 2 == 0 else -distance(k)


class Step:
    def __init__(self, refs):
        (self.tok_in, self.cot_in, self.wg_in, self.wu_in, self.wd_in,
         self.out, self.og, self.ou, self.od,
         self.tok, self.cot, self.wg, self.wu, self.wd, self.part, self.s1, self.g2, self.s2, self.back,
         self.tot, self.b1, self.b2, self.r1, self.r2, self.by, self.ry, self.bz, self.rz,
         self.vg, self.vu, self.vd, self.ht, self.send_sem, self.recv_sem, self.local_sem) = refs
        hid, mod = lax.axis_index("hid"), lax.axis_index("mod")
        self.x, self.yl, self.z = hid // 16, (hid // 8) % 2, hid % 8
        self.yh, self.c = mod // 2, mod % 2
        self.ids = {}
        self.sent = []
        self.n_local = 0
        self.local = []
        half = self.tok.shape[1] // 2
        self.half = (pl.ds(0, half), pl.ds(half, half))

    def dev(self, dx=0, dz=0, yl=None, yh=None, c=None):
        x = lax.rem(self.x + (dx + NX), NX)
        z = lax.rem(self.z + (dz + NZ), NZ)
        yl = self.yl if yl is None else yl
        yh = self.yh if yh is None else yh
        c = self.c if c is None else c
        return (x * 16 + yl * 8 + z, yh * 2 + c)

    def zchunk(self, k):
        return lax.rem(self.z + (offset(k) + NZ), NZ)

    def xblock(self, dx):
        return lax.rem(self.x + (dx + NX), NX)

    def rows(self, k, dx=None, y=None):
        base = self.zchunk(k) * CHUNK
        if dx is None:
            return pl.ds(pl.multiple_of(base, CHUNK), CHUNK)
        base = base + self.xblock(dx) * PAIR
        if y is None:
            return pl.ds(pl.multiple_of(base, PAIR), PAIR)
        return pl.ds(pl.multiple_of(base + y * SH, SH), SH)

    def side(self, k, c):
        return pl.ds(pl.multiple_of(self.zchunk(k) * CHUNK + c * 64, 64), 64)

    def sem(self, key):
        return self.ids.setdefault(key, len(self.ids))

    def send(self, key, src, dst, dev):
        i = self.sem(key)
        cp = pltpu.make_async_remote_copy(src_ref=src, dst_ref=dst, send_sem=self.send_sem.at[i],
                                          recv_sem=self.recv_sem.at[i], device_id=dev, device_id_type=MESH)
        cp.start()
        self.sent.append(cp)

    def wait(self, key, dst, dev):
        i = self.sem(key)
        pltpu.make_async_remote_copy(src_ref=dst, dst_ref=dst, send_sem=self.send_sem.at[i],
                                     recv_sem=self.recv_sem.at[i], device_id=dev, device_id_type=MESH).wait_recv()

    def fetch(self, src, dst):
        cp = pltpu.make_async_copy(src, dst, self.local_sem.at[self.n_local])
        self.n_local += 1
        cp.start()
        return cp

    def xd(self, q):
        return self.dev(dx=1 if q == 0 else -1)

    def zd(self, q):
        return self.dev(dz=1 if q == 0 else -1)

    def arr(self, a):
        return self.tok if a == "T" else self.cot

    def begin(self):
        own = self.rows(0, 0, self.yl)
        first = (self.fetch(self.tok_in, self.tok.at[own]), self.fetch(self.cot_in, self.cot.at[own]))
        self.weights = (self.fetch(self.wg_in, self.wg), self.fetch(self.wu_in, self.wu), self.fetch(self.wd_in, self.wd))
        bar = pltpu.get_barrier_semaphore()
        peers = [self.xd(0), self.xd(1), self.dev(yl=1 - self.yl), self.dev(yh=1 - self.yh), self.dev(c=1 - self.c)]
        peers += [self.zd(0), self.zd(1)]
        for p in peers:
            pl.semaphore_signal(bar, inc=1, device_id=p, device_id_type=MESH)
        pl.semaphore_wait(bar, len(peers))
        for cp in first:
            cp.wait()

    def plane(self, to, a, y, part):
        r = self.arr(a).at[self.rows(0, 0, y)]
        for q in (0, 1):
            if to == "x":
                self.send(("x0", a, q, part), r, r, self.xd(q))
            else:
                self.send(("z", 1 + q, a + "o", part), r, r, self.zd(q))

    def own(self):
        for a in "TC":
            r = self.arr(a).at[self.rows(0, 0, self.yl)]
            self.send(("y", a), r, r, self.dev(yl=1 - self.yl))
        for to, a in (("x", "T"), ("x", "C"), ("z", "C"), ("z", "T")):
            self.plane(to, a, self.yl, 0)

    def y(self):
        for a in "TC":
            self.wait(("y", a), self.arr(a).at[self.rows(0, 0, 1 - self.yl)], self.dev(yl=1 - self.yl))
        for to, a in (("x", "T"), ("x", "C"), ("z", "C"), ("z", "T")):
            self.plane(to, a, 1 - self.yl, 1)

    def x0(self, a, q):
        dx = -1 if q == 0 else 1
        for part, y in ((0, self.yl), (1, 1 - self.yl)):
            self.wait(("x0", a, q, part), self.arr(a).at[self.rows(0, dx, y)], self.xd(1 - q))
        r = self.arr(a).at[self.rows(0, dx)]
        h = self.arr(a).at[self.rows(0, dx), self.half[q]]
        self.send(("x0b", a, q), h, h, self.xd(q))
        if a == "T":
            for p in (0, 1):
                self.send(("z", 1 + p, "T%d" % (1 + q), 0), r, r, self.zd(p))

    def x0b(self, a):
        for q in (0, 1):
            self.wait(("x0b", a, q), self.arr(a).at[self.rows(0, 2), self.half[q]], self.xd(1 - q))
        if a == "T":
            r = self.tok.at[self.rows(0, 2)]
            for p in (0, 1):
                self.send(("z", 1 + p, "T3", 0), r, r, self.zd(p))

    def zin(self, k, p):
        d = 0 if k % 2 else 1
        a = self.arr(p[0])
        dx = {"": 0, "0": 0, "1": -1, "2": 1, "3": 2}[p[1:]]
        r = a.at[self.rows(k, dx)]
        if k == 7:
            for q in (0, 1):
                self.wait(("z", 7, p, q), a.at[self.rows(k, dx), self.half[q]], self.zd(1 - q))
        elif k <= 2 and dx == 0:
            for part, y in ((0, self.yl), (1, 1 - self.yl)):
                self.wait(("z", k, p[0] + "o", part), a.at[self.rows(k, dx, y)], self.zd(1 - d))
        else:
            self.wait(("z", k, p, 0), r, self.zd(1 - d))
        self.onward(k, p, dx)
        if p == "C" and k not in ZC:
            for q in (0, 1):
                self.send(("x", k, q), r, r, self.xd(q))

    def onward(self, k, p, dx):
        d = 0 if k % 2 else 1
        a = self.arr(p[0])
        if k < 5:
            r = a.at[self.rows(k, dx)]
            self.send(("z", k + 2, p, 0), r, r, self.zd(d))
        elif k < 7:
            h = a.at[self.rows(k, dx), self.half[d]]
            self.send(("z", 7, p, d), h, h, self.zd(d))

    def xin(self, k, q):
        dx = -1 if q == 0 else 1
        self.wait(("x", k, q), self.cot.at[self.rows(k, dx)], self.xd(1 - q))
        h = self.cot.at[self.rows(k, dx), self.half[q]]
        self.send(("xb", k, q), h, h, self.xd(q))
        if min(k + 2, 7) in ZC:
            self.onward(k, "C%d" % (1 + q), dx)

    def xb(self, k):
        for q in (0, 1):
            self.wait(("xb", k, q), self.cot.at[self.rows(k, 2), self.half[q]], self.xd(1 - q))
        if min(k + 2, 7) in ZC:
            self.onward(k, "C3", 2)

    def ready(self):
        for cp in self.weights:
            cp.wait()
        self.weights = ()

    def F(self, k):
        self.ready()
        r = self.rows(k)
        t = self.tok[r, :]
        self.part[k, 0] = lax.dot_general(t, self.wg[...], NT, preferred_element_type=F32)
        self.part[k, 1] = lax.dot_general(t, self.wu[...], NT, preferred_element_type=F32)
        self.part[k, 2] = lax.dot_general(self.cot[r, :], self.wd[...], NT, preferred_element_type=F32)
        other = pl.ds(pl.multiple_of((1 - self.c) * 64, 64), 64)
        self.send(("s1", k), self.part.at[k, :, other, :], self.s1.at[k], self.dev(c=1 - self.c))

    def G(self, k):
        self.wait(("s1", k), self.s1.at[k], self.dev(c=1 - self.c))
        mine = pl.ds(pl.multiple_of(self.c * 64, 64), 64)
        for i in range(3):
            total = self.part[k, i, mine, :] + self.s1[k, i]
            self.s1[k, i] = total
            self.g2[k, i] = total.astype(BF)
        self.send(("s2", k), self.g2.at[k], self.s2.at[k], self.dev(yh=1 - self.yh))

    def H(self, k):
        self.wait(("s2", k), self.s2.at[k], self.dev(yh=1 - self.yh))
        gate, up, grad = (self.s1[k, i] + self.s2[k, i].astype(F32) for i in range(3))
        s = jax.nn.sigmoid(gate)
        a = gate * s
        r = self.side(k, self.c)
        self.back[0, r, :] = (a * up).astype(BF)
        self.back[1, r, :] = (grad * up * (s * (1.0 + gate * (1.0 - s)))).astype(BF)
        self.back[2, r, :] = (grad * a).astype(BF)
        b = self.back.at[:, r, :]
        self.send(("s4", k), b, b, self.dev(c=1 - self.c))

    def J(self, k):
        self.wait(("s4", k), self.back.at[:, self.side(k, 1 - self.c), :], self.dev(c=1 - self.c))
        r = self.rows(k)
        self.tot[k] = jnp.dot(self.back[1, r, :], self.wg[...], preferred_element_type=F32) + jnp.dot(
            self.back[2, r, :], self.wu[...], preferred_element_type=F32
        )
        self.b1[k] = self.tot[k, self.block(2), :].astype(BF)
        if k in DIRECT:
            self.send(("r1", k), self.b1.at[k], self.r1.at[k], self.dev(dx=2))
            for q in (0, 1):
                self.b2[k, q] = self.tot[k, self.block(1 if q == 0 else -1), :].astype(BF)
                self.send(("r2", k, q), self.b2.at[k, q], self.r2.at[k, q], self.xd(q))
        else:
            for q in (0, 1):
                self.send(("r1", k, q), self.b1.at[k, :, self.half[q]], self.r1.at[k, :, self.half[q]], self.xd(q))

    def block(self, dx):
        return pl.ds(pl.multiple_of(self.xblock(dx) * PAIR, PAIR), PAIR)

    def K(self, k):
        for q in (0, 1):
            h, o = self.half[q], self.half[1 - q]
            self.wait(("r1", k, q), self.r1.at[k, :, h], self.xd(1 - q))
            b = self.block(1 if q == 0 else -1)
            self.b2[k, q, :, h] = (self.tot[k, b, h] + self.r1[k, :, h].astype(F32)).astype(BF)
            self.b2[k, q, :, o] = self.tot[k, b, o].astype(BF)
            self.send(("r2", k, q), self.b2.at[k, q], self.r2.at[k, q], self.xd(q))

    def L(self, k):
        for q in (0, 1):
            self.wait(("r2", k, q), self.r2.at[k, q], self.xd(1 - q))
        b = self.block(0)
        s = self.tot[k, b, :] + self.r2[k, 0].astype(F32) + self.r2[k, 1].astype(F32)
        if k in DIRECT:
            self.wait(("r1", k), self.r1.at[k], self.dev(dx=2))
            s = s + self.r1[k].astype(F32)
        self.tot[k, b, :] = s
        if k in FAR:
            for i, y in ((0, self.yl), (1, 1 - self.yl)):
                self.bz[k, i] = self.tot[k, self.yrows(y), :].astype(BF)
                self.send(("rz", k, i), self.bz.at[k, i], self.rz.at[k, i], self.dev(dz=offset(k), yl=y))
        else:
            self.by[k] = self.tot[k, self.yrows(1 - self.yl), :].astype(BF)
            self.send(("ry", k), self.by.at[k], self.ry.at[k], self.dev(yl=1 - self.yl))

    def yrows(self, y):
        return pl.ds(pl.multiple_of(self.xblock(0) * PAIR + y * SH, SH), SH)

    def M(self, k):
        self.wait(("ry", k), self.ry.at[k], self.dev(yl=1 - self.yl))
        s = self.tot[k, self.yrows(self.yl), :] + self.ry[k].astype(F32)
        if k == 0:
            self.tot[k, self.yrows(self.yl), :] = s
        else:
            self.bz[k, 0] = s.astype(BF)
            self.send(("rz", k, 0), self.bz.at[k, 0], self.rz.at[k, 0], self.dev(dz=offset(k)))

    def N(self):
        s = self.tot[0, self.yrows(self.yl), :]
        for k in range(1, NZ):
            for i, y in ((0, self.yl), (1, 1 - self.yl))[: 2 if k in FAR else 1]:
                self.wait(("rz", k, i), self.rz.at[k, i], self.dev(dz=-offset(k), yl=y))
                s = s + self.rz[k, i].astype(F32)
        self.out[...] = s.astype(BF)

    def turn(self):
        for i in range(3):
            self.ht[i] = self.back[i].T

    def W(self, j):
        n = self.tok.shape[1] // TILES
        cs = pl.ds(j * n, n)
        for i, a, v, o in ((1, self.tok, self.vg, self.og), (2, self.tok, self.vu, self.ou), (0, self.cot, self.vd, self.od)):
            v[:, cs] = jnp.dot(self.ht[i], a[:, cs], preferred_element_type=F32).astype(BF)
            self.local.append(self.fetch(v.at[:, cs], o.at[:, cs]))

    def finish(self):
        self.ready()
        for cp in self.sent:
            cp.wait_send()
        for cp in self.local:
            cp.wait()


NAMES = {"z": "zin", "x": "xin", "ht": "turn"}


def kernel(*refs):
    step = Step(refs)
    step.begin()
    for name, *args in ORDER:
        getattr(step, NAMES.get(name, name))(*args)
    step.finish()


def hand_over(*refs):
    for src, dst in zip(refs[:4], refs[4:]):
        dst[...] = src[...]


def shards(tokens, grad_output, gate_weight, up_weight, down_weight):
    d, f = gate_weight.shape
    n = NZ * CHUNK
    anywhere = pl.BlockSpec(memory_space=pl.ANY)
    vmem = pltpu.VMEM
    results = pl.pallas_call(
        kernel,
        out_shape=(
            jax.ShapeDtypeStruct((SH, d), BF),
            jax.ShapeDtypeStruct((f, d), BF),
            jax.ShapeDtypeStruct((f, d), BF),
            jax.ShapeDtypeStruct((f, d), BF),
        ),
        in_specs=[anywhere] * 5,
        out_specs=(pl.BlockSpec(memory_space=vmem), anywhere, anywhere, anywhere),
        scratch_shapes=[
            vmem((n, d), BF), vmem((n, d), BF),
            vmem((f, d), BF), vmem((f, d), BF), vmem((f, d), BF),
            vmem((NZ, 3, CHUNK, f), F32), vmem((NZ, 3, 64, f), F32), vmem((NZ, 3, 64, f), BF), vmem((NZ, 3, 64, f), BF),
            vmem((3, n, f), BF),
            vmem((NZ, CHUNK, d), F32),
            vmem((NZ, PAIR, d), BF), vmem((NZ, 2, PAIR, d), BF),
            vmem((NZ, PAIR, d), BF), vmem((NZ, 2, PAIR, d), BF),
            vmem((NZ, SH, d), BF), vmem((NZ, SH, d), BF), vmem((NZ, 2, SH, d), BF), vmem((NZ, 2, SH, d), BF),
            vmem((f, d), BF), vmem((f, d), BF), vmem((f, d), BF), vmem((3, f, n), BF),
            pltpu.SemaphoreType.DMA((200,)), pltpu.SemaphoreType.DMA((200,)), pltpu.SemaphoreType.DMA((5 + 3 * TILES,)),
        ],
        compiler_params=pltpu.CompilerParams(collective_id=0, has_side_effects=True, vmem_limit_bytes=62 << 20),
        cost_estimate=pl.CostEstimate(flops=16 * n * d * f, bytes_accessed=12 * d * f, transcendentals=n * f),
    )(tokens, grad_output, gate_weight.T, up_weight.T, down_weight)
    blocks = [pl.BlockSpec((SH, d), lambda i: (0, 0))] + [pl.BlockSpec((f // COPIES, d), lambda i: (i, 0))] * 3
    grad_tokens, grad_gate, grad_up, grad_down = pl.pallas_call(
        hand_over,
        grid=(COPIES,),
        out_shape=tuple(jax.ShapeDtypeStruct(r.shape, r.dtype) for r in results),
        in_specs=blocks,
        out_specs=tuple(blocks),
    )(*results)
    return grad_tokens, grad_gate.T, grad_up.T, grad_down


def solution(mesh):
    placed = (P("hid", "mod"), P("hid", "mod"), P("mod", "hid"), P("mod", "hid"), P("hid", "mod"))
    return jax.shard_map(
        shards,
        mesh=mesh,
        in_specs=placed,
        out_specs=(P("hid", "mod"), P("mod", "hid"), P("mod", "hid"), P("hid", "mod")),
        check_vma=False,
    )
```

```python
import functools

import jax
import jax.numpy as jnp
from jax import lax
from jax.experimental import pallas as pl
from jax.experimental.pallas import tpu as pltpu
from jax.sharding import PartitionSpec as P

MESH = pl.DeviceIdType.MESH
BF = jnp.bfloat16
F32 = jnp.float32
NT = (((1,), (1,)), ((), ()))

NX, NZ = 4, 8
SH = 16
PAIR = 2 * SH
CHUNK = NX * PAIR
TILES = 8
ZC = (7,)
TX = (3, 4, 5, 6, 7)
YF = (0,)
DIRECT = (7,)
FAR = (6, 7)

ORDER = (
    ('own',), ('y',), ('x0', 'T', 0), ('x0', 'T', 1), ('z', 1, 'C'), ('z', 2, 'C'), ('z', 1, 'T0'), ('z', 2, 'T0'),
    ('x0', 'C', 0), ('x0', 'C', 1), ('x0b', 'T'), ('z', 1, 'T1'), ('z', 2, 'T1'), ('x', 1, 0), ('x', 1, 1),
    ('z', 1, 'T2'), ('z', 2, 'T2'), ('x', 2, 0), ('x', 2, 1), ('z', 3, 'C'), ('z', 4, 'C'), ('x0b', 'C'), ('F', 0),
    ('xb', 1), ('z', 3, 'T0'), ('z', 4, 'T0'), ('xb', 2), ('G', 0), ('z', 1, 'T3'), ('z', 2, 'T3'), ('F', 1),
    ('x', 3, 0), ('x', 3, 1), ('F', 2), ('z', 3, 'T1'), ('z', 4, 'T1'), ('G', 1), ('x', 4, 0), ('x', 4, 1), ('H', 0),
    ('G', 2), ('xb', 3), ('z', 3, 'T2'), ('z', 4, 'T2'), ('J', 0), ('z', 5, 'C'), ('z', 6, 'C'), ('t3', 3), ('F', 3),
    ('xb', 4), ('H', 1), ('t3', 4), ('F', 4), ('z', 5, 'T0'), ('z', 6, 'T0'), ('G', 3), ('J', 1), ('H', 2),
    ('z', 5, 'T1'), ('z', 6, 'T1'), ('x', 5, 0), ('x', 5, 1), ('G', 4), ('J', 2), ('z', 5, 'T2'), ('z', 6, 'T2'),
    ('K', 1), ('z', 7, 'C'), ('x', 6, 0), ('x', 6, 1), ('Y', 0), ('z', 7, 'T0'), ('z', 7, 'T1'), ('xb', 5),
    ('t3', 5), ('F', 5), ('K', 2), ('t3', 6), ('z', 7, 'C1'), ('H', 3), ('G', 5), ('z', 7, 'T2'), ('z', 7, 'C2'),
    ('J', 3), ('L', 1), ('xb', 6), ('F', 6), ('K', 0), ('H', 4), ('G', 6), ('z', 7, 'C3'), ('J', 4), ('H', 5),
    ('L', 2), ('M', 1), ('t3', 7), ('K', 3), ('F', 7), ('J', 5), ('K', 4), ('G', 7), ('H', 6), ('L', 0), ('M', 2),
    ('J', 6), ('L', 3), ('K', 5), ('L', 4), ('H', 7), ('K', 6), ('M', 3), ('J', 7), ('ht',), ('L', 5), ('M', 4),
    ('W', 0), ('W', 1), ('L', 6), ('M', 5), ('W', 2), ('W', 3), ('W', 4), ('L', 7), ('W', 5), ('W', 6), ('W', 7),
    ('N',),
)


def distance(k):
    return (k + 1) // 2


def offset(k):
    return distance(k) if k % 2 == 0 else -distance(k)


class Step:
    def __init__(self, refs):
        (self.tok_in, self.cot_in, self.wg_in, self.wu_in, self.wd_in,
         self.out, self.og, self.ou, self.od,
         self.tok, self.cot, self.wg, self.wu, self.wd, self.part, self.s1, self.g2, self.s2, self.back,
         self.tot, self.b1, self.b2, self.r1, self.r2, self.by, self.ry, self.bz, self.rz, self.by4, self.ry4,
         self.ht, self.send_sem, self.recv_sem, self.local_sem) = refs
        hid, mod = lax.axis_index("hid"), lax.axis_index("mod")
        self.x, self.yl, self.z = hid // 16, (hid // 8) % 2, hid % 8
        self.yh, self.c = mod // 2, mod % 2
        self.ids = {}
        self.sent = []
        self.n_local = 0
        half = self.tok.shape[1] // 2
        self.half = (pl.ds(0, half), pl.ds(half, half))

    def dev(self, dx=0, dz=0, yl=None, yh=None, c=None):
        x = lax.rem(self.x + (dx + NX), NX)
        z = lax.rem(self.z + (dz + NZ), NZ)
        yl = self.yl if yl is None else yl
        yh = self.yh if yh is None else yh
        c = self.c if c is None else c
        return (x * 16 + yl * 8 + z, yh * 2 + c)

    def zchunk(self, k):
        return lax.rem(self.z + (offset(k) + NZ), NZ)

    def xblock(self, dx):
        return lax.rem(self.x + (dx + NX), NX)

    def rows(self, k, dx=None, y=None):
        base = self.zchunk(k) * CHUNK
        if dx is None:
            return pl.ds(pl.multiple_of(base, CHUNK), CHUNK)
        base = base + self.xblock(dx) * PAIR
        if y is None:
            return pl.ds(pl.multiple_of(base, PAIR), PAIR)
        return pl.ds(pl.multiple_of(base + y * SH, SH), SH)

    def side(self, k, c):
        return pl.ds(pl.multiple_of(self.zchunk(k) * CHUNK + c * 64, 64), 64)

    def sem(self, key):
        return self.ids.setdefault(key, len(self.ids))

    def send(self, key, src, dst, dev):
        i = self.sem(key)
        cp = pltpu.make_async_remote_copy(src_ref=src, dst_ref=dst, send_sem=self.send_sem.at[i],
                                          recv_sem=self.recv_sem.at[i], device_id=dev, device_id_type=MESH)
        cp.start()
        self.sent.append(cp)

    def wait(self, key, dst, dev):
        i = self.sem(key)
        pltpu.make_async_remote_copy(src_ref=dst, dst_ref=dst, send_sem=self.send_sem.at[i],
                                     recv_sem=self.recv_sem.at[i], device_id=dev, device_id_type=MESH).wait_recv()

    def fetch(self, src, dst):
        cp = pltpu.make_async_copy(src, dst, self.local_sem.at[self.n_local])
        self.n_local += 1
        cp.start()
        return cp

    def xd(self, q):
        return self.dev(dx=1 if q == 0 else -1)

    def zd(self, q):
        return self.dev(dz=1 if q == 0 else -1)

    def arr(self, a):
        return self.tok if a == "T" else self.cot

    def begin(self):
        own = self.rows(0, 0, self.yl)
        first = (self.fetch(self.tok_in, self.tok.at[own]), self.fetch(self.cot_in, self.cot.at[own]))
        self.weights = (self.fetch(self.wg_in, self.wg), self.fetch(self.wu_in, self.wu), self.fetch(self.wd_in, self.wd))
        bar = pltpu.get_barrier_semaphore()
        peers = [self.xd(0), self.xd(1), self.dev(yl=1 - self.yl), self.dev(yh=1 - self.yh), self.dev(c=1 - self.c)]
        peers += [self.zd(0), self.zd(1)]
        for p in peers:
            pl.semaphore_signal(bar, inc=1, device_id=p, device_id_type=MESH)
        pl.semaphore_wait(bar, len(peers))
        for cp in first:
            cp.wait()

    def plane(self, to, a, y, part):
        r = self.arr(a).at[self.rows(0, 0, y)]
        for q in (0, 1):
            if to == "x":
                self.send(("x0", a, q, part), r, r, self.xd(q))
            else:
                self.send(("z", 1 + q, a + "o", part), r, r, self.zd(q))

    def own(self):
        for a in "TC":
            r = self.arr(a).at[self.rows(0, 0, self.yl)]
            self.send(("y", a), r, r, self.dev(yl=1 - self.yl))
        for to, a in (("x", "T"), ("x", "C"), ("z", "C"), ("z", "T")):
            self.plane(to, a, self.yl, 0)

    def y(self):
        for a in "TC":
            self.wait(("y", a), self.arr(a).at[self.rows(0, 0, 1 - self.yl)], self.dev(yl=1 - self.yl))
        for to, a in (("x", "T"), ("x", "C"), ("z", "C"), ("z", "T")):
            self.plane(to, a, 1 - self.yl, 1)

    def x0(self, a, q):
        dx = -1 if q == 0 else 1
        for part, y in ((0, self.yl), (1, 1 - self.yl)):
            self.wait(("x0", a, q, part), self.arr(a).at[self.rows(0, dx, y)], self.xd(1 - q))
        r = self.arr(a).at[self.rows(0, dx)]
        h = self.arr(a).at[self.rows(0, dx), self.half[q]]
        self.send(("x0b", a, q), h, h, self.xd(q))
        if a == "T":
            for p in (0, 1):
                self.send(("z", 1 + p, "T%d" % (1 + q), 0), r, r, self.zd(p))

    def x0b(self, a):
        for q in (0, 1):
            self.wait(("x0b", a, q), self.arr(a).at[self.rows(0, 2), self.half[q]], self.xd(1 - q))
        if a == "T":
            r = self.tok.at[self.rows(0, 2)]
            for p in (0, 1):
                if 1 + p not in TX:
                    self.send(("z", 1 + p, "T3", 0), r, r, self.zd(p))

    def zin(self, k, p):
        d = 0 if k % 2 else 1
        a = self.arr(p[0])
        dx = {"": 0, "0": 0, "1": -1, "2": 1, "3": 2}[p[1:]]
        r = a.at[self.rows(k, dx)]
        if k == 7:
            for q in (0, 1):
                self.wait(("z", 7, p, q), a.at[self.rows(k, dx), self.half[q]], self.zd(1 - q))
        elif k <= 2 and dx == 0:
            for part, y in ((0, self.yl), (1, 1 - self.yl)):
                self.wait(("z", k, p[0] + "o", part), a.at[self.rows(k, dx, y)], self.zd(1 - d))
        else:
            self.wait(("z", k, p, 0), r, self.zd(1 - d))
        if p != "T3" or min(k + 2, 7) not in TX:
            self.onward(k, p, dx)
        if k in TX and p in ("T1", "T2"):
            q = 0 if p == "T1" else 1
            h = a.at[self.rows(k, dx), self.half[q]]
            self.send(("t3", k, q), h, h, self.xd(q))
        if p == "C" and k not in ZC:
            for q in (0, 1):
                self.send(("x", k, q), r, r, self.xd(q))

    def onward(self, k, p, dx):
        d = 0 if k % 2 else 1
        a = self.arr(p[0])
        if k < 5:
            r = a.at[self.rows(k, dx)]
            self.send(("z", k + 2, p, 0), r, r, self.zd(d))
        elif k < 7:
            h = a.at[self.rows(k, dx), self.half[d]]
            self.send(("z", 7, p, d), h, h, self.zd(d))

    def t3(self, k):
        for q in (0, 1):
            self.wait(("t3", k, q), self.tok.at[self.rows(k, 2), self.half[q]], self.xd(1 - q))
        if min(k + 2, 7) not in TX:
            self.onward(k, "T3", 2)

    def xin(self, k, q):
        dx = -1 if q == 0 else 1
        self.wait(("x", k, q), self.cot.at[self.rows(k, dx)], self.xd(1 - q))
        h = self.cot.at[self.rows(k, dx), self.half[q]]
        self.send(("xb", k, q), h, h, self.xd(q))
        if min(k + 2, 7) in ZC:
            self.onward(k, "C%d" % (1 + q), dx)

    def xb(self, k):
        for q in (0, 1):
            self.wait(("xb", k, q), self.cot.at[self.rows(k, 2), self.half[q]], self.xd(1 - q))
        if min(k + 2, 7) in ZC:
            self.onward(k, "C3", 2)

    def ready(self):
        for cp in self.weights:
            cp.wait()
        self.weights = ()

    def F(self, k):
        self.ready()
        r = self.rows(k)
        t = self.tok[r, :]
        self.part[k, 0] = lax.dot_general(t, self.wg[...], NT, preferred_element_type=F32)
        self.part[k, 1] = lax.dot_general(t, self.wu[...], NT, preferred_element_type=F32)
        self.part[k, 2] = lax.dot_general(self.cot[r, :], self.wd[...], NT, preferred_element_type=F32)
        other = pl.ds(pl.multiple_of((1 - self.c) * 64, 64), 64)
        self.send(("s1", k), self.part.at[k, :, other, :], self.s1.at[k], self.dev(c=1 - self.c))

    def G(self, k):
        self.wait(("s1", k), self.s1.at[k], self.dev(c=1 - self.c))
        mine = pl.ds(pl.multiple_of(self.c * 64, 64), 64)
        for i in range(3):
            total = self.part[k, i, mine, :] + self.s1[k, i]
            self.s1[k, i] = total
            self.g2[k, i] = total.astype(BF)
        self.send(("s2", k), self.g2.at[k], self.s2.at[k], self.dev(yh=1 - self.yh))

    def H(self, k):
        self.wait(("s2", k), self.s2.at[k], self.dev(yh=1 - self.yh))
        gate, up, grad = (self.s1[k, i] + self.s2[k, i].astype(F32) for i in range(3))
        s = jax.nn.sigmoid(gate)
        a = gate * s
        r = self.side(k, self.c)
        self.back[0, r, :] = (a * up).astype(BF)
        self.back[1, r, :] = (grad * up * (s * (1.0 + gate * (1.0 - s)))).astype(BF)
        self.back[2, r, :] = (grad * a).astype(BF)
        b = self.back.at[:, r, :]
        self.send(("s4", k), b, b, self.dev(c=1 - self.c))

    def J(self, k):
        self.wait(("s4", k), self.back.at[:, self.side(k, 1 - self.c), :], self.dev(c=1 - self.c))
        r = self.rows(k)
        self.tot[k] = jnp.dot(self.back[1, r, :], self.wg[...], preferred_element_type=F32) + jnp.dot(
            self.back[2, r, :], self.wu[...], preferred_element_type=F32
        )
        if k in YF:
            i = YF.index(k)
            for b in range(NX):
                self.by4[i, b * SH : (b + 1) * SH] = self.tot[k, self.strip(b, 1 - self.yl), :].astype(BF)
            self.send(("ry", k), self.by4.at[i], self.ry4.at[i], self.dev(yl=1 - self.yl))
        else:
            self.over_x(k)

    def strip(self, b, y):
        return pl.ds(pl.multiple_of(b * PAIR + y * SH, SH), SH)

    def Y(self, k):
        i = YF.index(k)
        self.wait(("ry", k), self.ry4.at[i], self.dev(yl=1 - self.yl))
        for b in range(NX):
            r = self.strip(b, self.yl)
            self.tot[k, r, :] = self.tot[k, r, :] + self.ry4[i, b * SH : (b + 1) * SH].astype(F32)
        self.over_x(k)

    def block(self, k, dx):
        if k in YF:
            return self.strip(self.xblock(dx), self.yl)
        return pl.ds(pl.multiple_of(self.xblock(dx) * PAIR, PAIR), PAIR)

    def over_x(self, k):
        n = pl.ds(0, SH if k in YF else PAIR)
        self.b1[k, n] = self.tot[k, self.block(k, 2), :].astype(BF)
        if k in DIRECT:
            self.send(("r1", k), self.b1.at[k, n], self.r1.at[k, n], self.dev(dx=2))
            for q in (0, 1):
                self.b2[k, q, n] = self.tot[k, self.block(k, 1 if q == 0 else -1), :].astype(BF)
                self.send(("r2", k, q), self.b2.at[k, q, n], self.r2.at[k, q, n], self.xd(q))
        else:
            for q in (0, 1):
                self.send(("r1", k, q), self.b1.at[k, n, self.half[q]], self.r1.at[k, n, self.half[q]], self.xd(q))

    def K(self, k):
        n = pl.ds(0, SH if k in YF else PAIR)
        for q in (0, 1):
            h, o = self.half[q], self.half[1 - q]
            self.wait(("r1", k, q), self.r1.at[k, n, h], self.xd(1 - q))
            b = self.block(k, 1 if q == 0 else -1)
            self.b2[k, q, n, h] = (self.tot[k, b, h] + self.r1[k, n, h].astype(F32)).astype(BF)
            self.b2[k, q, n, o] = self.tot[k, b, o].astype(BF)
            self.send(("r2", k, q), self.b2.at[k, q, n], self.r2.at[k, q, n], self.xd(q))

    def L(self, k):
        n = pl.ds(0, SH if k in YF else PAIR)
        for q in (0, 1):
            self.wait(("r2", k, q), self.r2.at[k, q, n], self.xd(1 - q))
        b = self.block(k, 0)
        s = self.tot[k, b, :] + self.r2[k, 0, n].astype(F32) + self.r2[k, 1, n].astype(F32)
        if k in DIRECT:
            self.wait(("r1", k), self.r1.at[k, n], self.dev(dx=2))
            s = s + self.r1[k, n].astype(F32)
        if k in YF:
            self.over_z(k, s)
            return
        self.tot[k, b, :] = s
        if k in FAR:
            for i, y in ((0, self.yl), (1, 1 - self.yl)):
                self.bz[k, i] = self.tot[k, self.yrows(y), :].astype(BF)
                self.send(("rz", k, i), self.bz.at[k, i], self.rz.at[k, i], self.dev(dz=offset(k), yl=y))
        else:
            self.by[k] = self.tot[k, self.yrows(1 - self.yl), :].astype(BF)
            self.send(("ry", k), self.by.at[k], self.ry.at[k], self.dev(yl=1 - self.yl))

    def yrows(self, y):
        return self.strip(self.xblock(0), y)

    def over_z(self, k, s):
        if k == 0:
            self.tot[k, self.yrows(self.yl), :] = s
        else:
            self.bz[k, 0] = s.astype(BF)
            self.send(("rz", k, 0), self.bz.at[k, 0], self.rz.at[k, 0], self.dev(dz=offset(k)))

    def M(self, k):
        self.wait(("ry", k), self.ry.at[k], self.dev(yl=1 - self.yl))
        self.over_z(k, self.tot[k, self.yrows(self.yl), :] + self.ry[k].astype(F32))

    def N(self):
        s = self.tot[0, self.yrows(self.yl), :]
        for k in range(1, NZ):
            for i, y in ((0, self.yl), (1, 1 - self.yl))[: 2 if k in FAR and k not in YF else 1]:
                self.wait(("rz", k, i), self.rz.at[k, i], self.dev(dz=-offset(k), yl=y))
                s = s + self.rz[k, i].astype(F32)
        self.out[...] = s.astype(BF)

    def turn(self):
        for i in range(3):
            self.ht[i] = self.back[i].T

    def W(self, j):
        n = self.tok.shape[1] // TILES
        cs = pl.ds(j * n, n)
        for i, a, o in ((1, self.tok, self.og), (2, self.tok, self.ou), (0, self.cot, self.od)):
            o[:, cs] = jnp.dot(self.ht[i], a[:, cs], preferred_element_type=F32).astype(BF)

    def finish(self):
        self.ready()
        for cp in self.sent:
            cp.wait_send()


NAMES = {"z": "zin", "x": "xin", "ht": "turn"}


def kernel(*refs):
    step = Step(refs)
    step.begin()
    for name, *args in ORDER:
        getattr(step, NAMES.get(name, name))(*args)
    step.finish()


def shards(tokens, grad_output, gate_weight, up_weight, down_weight):
    d, f = gate_weight.shape
    n = NZ * CHUNK
    anywhere = pl.BlockSpec(memory_space=pl.ANY)
    vmem = pltpu.VMEM
    grad_tokens, grad_gate, grad_up, grad_down = pl.pallas_call(
        kernel,
        out_shape=(
            jax.ShapeDtypeStruct((SH, d), BF),
            vmem((f, d), BF),
            vmem((f, d), BF),
            vmem((f, d), BF),
        ),
        in_specs=[anywhere] * 5,
        out_specs=(pl.BlockSpec(memory_space=vmem),) * 4,
        scratch_shapes=[
            vmem((n, d), BF), vmem((n, d), BF),
            vmem((f, d), BF), vmem((f, d), BF), vmem((f, d), BF),
            vmem((NZ, 3, CHUNK, f), F32), vmem((NZ, 3, 64, f), F32), vmem((NZ, 3, 64, f), BF), vmem((NZ, 3, 64, f), BF),
            vmem((3, n, f), BF),
            vmem((NZ, CHUNK, d), F32),
            vmem((NZ, PAIR, d), BF), vmem((NZ, 2, PAIR, d), BF),
            vmem((NZ, PAIR, d), BF), vmem((NZ, 2, PAIR, d), BF),
            vmem((NZ, SH, d), BF), vmem((NZ, SH, d), BF), vmem((NZ, 2, SH, d), BF), vmem((NZ, 2, SH, d), BF),
            vmem((max(1, len(YF)), NX * SH, d), BF), vmem((max(1, len(YF)), NX * SH, d), BF),
            vmem((3, f, n), BF),
            pltpu.SemaphoreType.DMA((200,)), pltpu.SemaphoreType.DMA((200,)), pltpu.SemaphoreType.DMA((5,)),
        ],
        compiler_params=pltpu.CompilerParams(collective_id=0, has_side_effects=True, vmem_limit_bytes=57 << 20),
        cost_estimate=pl.CostEstimate(flops=16 * n * d * f, bytes_accessed=12 * d * f, transcendentals=n * f),
    )(tokens, grad_output, gate_weight.T, up_weight.T, down_weight)
    return grad_tokens, grad_gate.T, grad_up.T, grad_down


def solution(mesh):
    placed = (P("hid", "mod"), P("hid", "mod"), P("mod", "hid"), P("mod", "hid"), P("hid", "mod"))
    return jax.shard_map(
        shards,
        mesh=mesh,
        in_specs=placed,
        out_specs=(P("hid", "mod"), P("mod", "hid"), P("mod", "hid"), P("hid", "mod")),
        check_vma=False,
    )
```

```python
import functools

import jax
import jax.numpy as jnp
from jax import lax
from jax.experimental import pallas as pl
from jax.experimental.pallas import tpu as pltpu
from jax.sharding import PartitionSpec as P

MESH = pl.DeviceIdType.MESH
BF = jnp.bfloat16
F32 = jnp.float32
NT = (((1,), (1,)), ((), ()))

NX, NZ = 4, 8
SH = 16
PAIR = 2 * SH
CHUNK = NX * PAIR
TILES = 8
ZC = (7,)
TX = (1, 2, 3, 6)
YC = (0, 1, 4)
YF = (2, 6)
DIRECT = (2, 6, 7)
FAR = (5,)

ORDER = (
    ('own',), ('y',), ('x0', 'C', 0), ('x0', 'C', 1), ('x0', 'T', 0), ('x0', 'T', 1), ('z', 1, 'C'), ('z', 2, 'C'),
    ('cx', 2), ('x0b', 'C'), ('cx', 1), ('z', 1, 'T0'), ('z', 2, 'T0'), ('x0b', 'T'), ('yc', 0), ('F', 0),
    ('z', 1, 'T1'), ('z', 2, 'T1'), ('x', 2, 0), ('x', 2, 1), ('G', 0), ('z', 1, 'T2'), ('x', 1, 0), ('x', 1, 1),
    ('z', 2, 'T2'), ('z', 3, 'C'), ('z', 4, 'C'), ('cx', 4), ('cx', 3), ('t3', 1), ('xb', 2), ('xb', 1),
    ('z', 3, 'T0'), ('z', 4, 'T0'), ('t3', 2), ('H', 0), ('x', 4, 0), ('F', 2), ('x', 4, 1), ('J', 0),
    ('z', 3, 'T1'), ('z', 4, 'T1'), ('yc', 1), ('G', 2), ('x', 3, 0), ('x', 3, 1), ('F', 1), ('z', 3, 'T2'),
    ('z', 4, 'T2'), ('xb', 4), ('K', 0), ('G', 1), ('z', 5, 'C'), ('z', 6, 'C'), ('cx', 5), ('cx', 6), ('t3', 3),
    ('xb', 3), ('F', 3), ('z', 5, 'T0'), ('z', 6, 'T0'), ('H', 2), ('yc', 4), ('L', 0), ('G', 3), ('J', 2),
    ('z', 4, 'T3'), ('F', 4), ('z', 5, 'T1'), ('z', 5, 'T2'), ('z', 6, 'T1'), ('x', 5, 0), ('x', 5, 1), ('H', 1),
    ('M', 0), ('G', 4), ('x', 6, 0), ('x', 6, 1), ('J', 1), ('z', 6, 'T2'), ('H', 3), ('z', 5, 'T3'), ('z', 7, 'C'),
    ('xb', 5), ('F', 5), ('z', 7, 'T0'), ('xb', 6), ('J', 3), ('z', 7, 'T1'), ('K', 1), ('t3', 6), ('F', 6),
    ('z', 7, 'C1'), ('Y', 2), ('G', 5), ('z', 7, 'T2'), ('z', 7, 'C2'), ('K', 3), ('G', 6), ('H', 4), ('z', 7, 'T3'),
    ('z', 7, 'C3'), ('F', 7), ('J', 4), ('G', 7), ('H', 5), ('L', 1), ('L', 2), ('J', 5), ('L', 3), ('H', 6),
    ('K', 4), ('J', 6), ('K', 5), ('H', 7), ('M', 1), ('J', 7), ('M', 3), ('ht',), ('L', 4), ('W', 0), ('L', 5),
    ('W', 1), ('W', 2), ('Y', 6), ('W', 3), ('L', 7), ('M', 4), ('W', 4), ('W', 5), ('L', 6), ('M', 7), ('W', 6),
    ('W', 7), ('N',),
)


def distance(k):
    return (k + 1) // 2


def offset(k):
    return distance(k) if k % 2 == 0 else -distance(k)


class Step:
    def __init__(self, refs):
        (self.tok_in, self.cot_in, self.wg_in, self.wu_in, self.wd_in,
         self.out, self.og, self.ou, self.od,
         self.tok, self.cot, self.wg, self.wu, self.wd, self.part, self.s1, self.g2, self.s2, self.back,
         self.tot, self.b1, self.b2, self.r1, self.r2, self.by, self.ry, self.bz, self.rz, self.by4, self.ry4,
         self.ht, self.send_sem, self.recv_sem, self.local_sem) = refs
        hid, mod = lax.axis_index("hid"), lax.axis_index("mod")
        self.x, self.yl, self.z = hid // 16, (hid // 8) % 2, hid % 8
        self.yh, self.c = mod // 2, mod % 2
        self.ids = {}
        self.sent = []
        self.n_local = 0
        half = self.tok.shape[1] // 2
        self.half = (pl.ds(0, half), pl.ds(half, half))

    def dev(self, dx=0, dz=0, yl=None, yh=None, c=None):
        x = lax.rem(self.x + (dx + NX), NX)
        z = lax.rem(self.z + (dz + NZ), NZ)
        yl = self.yl if yl is None else yl
        yh = self.yh if yh is None else yh
        c = self.c if c is None else c
        return (x * 16 + yl * 8 + z, yh * 2 + c)

    def zchunk(self, k):
        return lax.rem(self.z + (offset(k) + NZ), NZ)

    def xblock(self, dx):
        return lax.rem(self.x + (dx + NX), NX)

    def rows(self, k, dx=None, y=None):
        base = self.zchunk(k) * CHUNK
        if dx is None:
            return pl.ds(pl.multiple_of(base, CHUNK), CHUNK)
        base = base + self.xblock(dx) * PAIR
        if y is None:
            return pl.ds(pl.multiple_of(base, PAIR), PAIR)
        return pl.ds(pl.multiple_of(base + y * SH, SH), SH)

    def side(self, k, c):
        return pl.ds(pl.multiple_of(self.zchunk(k) * CHUNK + c * 64, 64), 64)

    def sem(self, key):
        return self.ids.setdefault(key, len(self.ids))

    def send(self, key, src, dst, dev):
        i = self.sem(key)
        cp = pltpu.make_async_remote_copy(src_ref=src, dst_ref=dst, send_sem=self.send_sem.at[i],
                                          recv_sem=self.recv_sem.at[i], device_id=dev, device_id_type=MESH)
        cp.start()
        self.sent.append(cp)

    def wait(self, key, dst, dev):
        i = self.sem(key)
        pltpu.make_async_remote_copy(src_ref=dst, dst_ref=dst, send_sem=self.send_sem.at[i],
                                     recv_sem=self.recv_sem.at[i], device_id=dev, device_id_type=MESH).wait_recv()

    def fetch(self, src, dst):
        cp = pltpu.make_async_copy(src, dst, self.local_sem.at[self.n_local])
        self.n_local += 1
        cp.start()
        return cp

    def xd(self, q):
        return self.dev(dx=1 if q == 0 else -1)

    def zd(self, q):
        return self.dev(dz=1 if q == 0 else -1)

    def arr(self, a):
        return self.tok if a == "T" else self.cot

    def begin(self):
        own = self.rows(0, 0, self.yl)
        first = (self.fetch(self.tok_in, self.tok.at[own]), self.fetch(self.cot_in, self.cot.at[own]))
        self.weights = (self.fetch(self.wg_in, self.wg), self.fetch(self.wu_in, self.wu), self.fetch(self.wd_in, self.wd))
        bar = pltpu.get_barrier_semaphore()
        peers = [self.xd(0), self.xd(1), self.dev(yl=1 - self.yl), self.dev(yh=1 - self.yh), self.dev(c=1 - self.c)]
        peers += [self.zd(0), self.zd(1)]
        for p in peers:
            pl.semaphore_signal(bar, inc=1, device_id=p, device_id_type=MESH)
        pl.semaphore_wait(bar, len(peers))
        for cp in first:
            cp.wait()

    def plane(self, to, a, y, part):
        r = self.arr(a).at[self.rows(0, 0, y)]
        for q in (0, 1):
            if to == "x":
                self.send(("x0", a, q, part), r, r, self.xd(q))
            else:
                self.send(("z", 1 + q, a + "o", part), r, r, self.zd(q))

    def own(self):
        for a in "TC":
            r = self.arr(a).at[self.rows(0, 0, self.yl)]
            self.send(("y", a), r, r, self.dev(yl=1 - self.yl))
        for to, a in (("x", "T"), ("x", "C"), ("z", "C"), ("z", "T")):
            self.plane(to, a, self.yl, 0)

    def y(self):
        for a in "TC":
            self.wait(("y", a), self.arr(a).at[self.rows(0, 0, 1 - self.yl)], self.dev(yl=1 - self.yl))
        for to, a in (("x", "T"), ("x", "C"), ("z", "C"), ("z", "T")):
            if (to, a) != ("x", "C") or 0 not in YC:
                self.plane(to, a, 1 - self.yl, 1)

    def x0(self, a, q):
        dx = -1 if q == 0 else 1
        ys = (self.yl, 1 - self.yl)
        if a == "C" and 0 in YC:
            ys = ys[:1]
        for part, y in enumerate(ys):
            self.wait(("x0", a, q, part), self.arr(a).at[self.rows(0, dx, y)], self.xd(1 - q))
        rows = self.crows(0, dx) if a == "C" else self.rows(0, dx)
        r = self.arr(a).at[rows]
        h = self.arr(a).at[rows, self.half[q]]
        self.send(("x0b", a, q), h, h, self.xd(q))
        if a == "T":
            for p in (0, 1):
                self.send(("z", 1 + p, "T%d" % (1 + q), 0), r, r, self.zd(p))
        else:
            self.gathered(0, q, dx, r)

    def x0b(self, a):
        rows = self.crows(0, 2) if a == "C" else self.rows(0, 2)
        for q in (0, 1):
            self.wait(("x0b", a, q), self.arr(a).at[rows, self.half[q]], self.xd(1 - q))
        r = self.arr(a).at[rows]
        if a == "T":
            for p in (0, 1):
                if 1 + p not in TX:
                    self.send(("z", 1 + p, "T3", 0), r, r, self.zd(p))
        else:
            self.gathered(0, 2, 2, r)

    def zin(self, k, p):
        d = 0 if k % 2 else 1
        a = self.arr(p[0])
        dx = {"": 0, "0": 0, "1": -1, "2": 1, "3": 2}[p[1:]]
        r = a.at[self.rows(k, dx)]
        if k == 7:
            for q in (0, 1):
                self.wait(("z", 7, p, q), a.at[self.rows(k, dx), self.half[q]], self.zd(1 - q))
        elif k <= 2 and dx == 0:
            for part, y in ((0, self.yl), (1, 1 - self.yl)):
                self.wait(("z", k, p[0] + "o", part), a.at[self.rows(k, dx, y)], self.zd(1 - d))
        else:
            self.wait(("z", k, p, 0), r, self.zd(1 - d))
        if p != "T3" or min(k + 2, 7) not in TX:
            self.onward(k, p, dx)
        if k in TX and p in ("T1", "T2"):
            q = 0 if p == "T1" else 1
            h = a.at[self.rows(k, dx), self.half[q]]
            self.send(("t3", k, q), h, h, self.xd(q))

    def onward(self, k, p, dx):
        d = 0 if k % 2 else 1
        a = self.arr(p[0])
        if k < 5:
            r = a.at[self.rows(k, dx)]
            self.send(("z", k + 2, p, 0), r, r, self.zd(d))
        elif k < 7:
            h = a.at[self.rows(k, dx), self.half[d]]
            self.send(("z", 7, p, d), h, h, self.zd(d))

    def t3(self, k):
        for q in (0, 1):
            self.wait(("t3", k, q), self.tok.at[self.rows(k, 2), self.half[q]], self.xd(1 - q))
        if min(k + 2, 7) not in TX:
            self.onward(k, "T3", 2)

    def crows(self, k, dx):
        return self.rows(k, dx, self.yl if k in YC else None)

    def cx(self, k):
        r = self.cot.at[self.crows(k, 0)]
        for q in (0, 1):
            self.send(("x", k, q), r, r, self.xd(q))

    def xin(self, k, q):
        dx = -1 if q == 0 else 1
        r = self.cot.at[self.crows(k, dx)]
        self.wait(("x", k, q), r, self.xd(1 - q))
        h = self.cot.at[self.crows(k, dx), self.half[q]]
        self.send(("xb", k, q), h, h, self.xd(q))
        self.gathered(k, q, dx, r)

    def xb(self, k):
        for q in (0, 1):
            self.wait(("xb", k, q), self.cot.at[self.crows(k, 2), self.half[q]], self.xd(1 - q))
        self.gathered(k, 2, 2, self.cot.at[self.crows(k, 2)])

    def gathered(self, k, i, dx, r):
        if k in YC:
            self.send(("yc", k, i), r, r, self.dev(yl=1 - self.yl))
        elif k and min(k + 2, 7) in ZC:
            self.onward(k, "C%d" % (1 + i), dx)

    def yc(self, k):
        for i, dx in enumerate((-1, 1, 2)):
            self.wait(("yc", k, i), self.cot.at[self.rows(k, dx, 1 - self.yl)], self.dev(yl=1 - self.yl))
        if k and min(k + 2, 7) in ZC:
            for i, dx in enumerate((-1, 1, 2)):
                self.onward(k, "C%d" % (1 + i), dx)

    def ready(self):
        for cp in self.weights:
            cp.wait()
        self.weights = ()

    def F(self, k):
        self.ready()
        r = self.rows(k)
        t = self.tok[r, :]
        self.part[k, 0] = lax.dot_general(t, self.wg[...], NT, preferred_element_type=F32)
        self.part[k, 1] = lax.dot_general(t, self.wu[...], NT, preferred_element_type=F32)
        self.part[k, 2] = lax.dot_general(self.cot[r, :], self.wd[...], NT, preferred_element_type=F32)
        other = pl.ds(pl.multiple_of((1 - self.c) * 64, 64), 64)
        self.send(("s1", k), self.part.at[k, :, other, :], self.s1.at[k], self.dev(c=1 - self.c))

    def G(self, k):
        self.wait(("s1", k), self.s1.at[k], self.dev(c=1 - self.c))
        mine = pl.ds(pl.multiple_of(self.c * 64, 64), 64)
        rest = []
        for i in range(3):
            total = self.part[k, i, mine, :] + self.s1[k, i]
            self.s1[k, i] = total
            low = total.astype(BF)
            for t in range(3):
                self.g2[k, (i * 3 + t) * 64 : (i * 3 + t + 1) * 64, :] = low[:, t * 128 : (t + 1) * 128]
            rest.append(low[:, 384:])
        self.g2[k, 576:640, :] = jnp.concatenate(rest[:2], axis=1)
        self.g2[k, 640:, :] = jnp.concatenate([rest[2][:32], rest[2][32:]], axis=1)
        self.send(("s2", k), self.g2.at[k], self.s2.at[k], self.dev(yh=1 - self.yh))

    def H(self, k):
        self.wait(("s2", k), self.s2.at[k], self.dev(yh=1 - self.yh))
        r = self.side(k, self.c)
        pair, last = self.s2[k, 576:640, :], self.s2[k, 640:, :]
        rest = (pair[:, :64], pair[:, 64:], jnp.concatenate([last[:, :64], last[:, 64:]], axis=0))
        for t in range(4):
            cs = pl.ds(t * 128, 128 if t < 3 else 64)
            far = [self.s2[k, (i * 3 + t) * 64 : (i * 3 + t + 1) * 64, :] if t < 3 else rest[i] for i in range(3)]
            gate, up, grad = (self.s1[k, i, :, cs] + far[i].astype(F32) for i in range(3))
            s = jax.nn.sigmoid(gate)
            a = gate * s
            self.back[0, r, cs] = (a * up).astype(BF)
            self.back[1, r, cs] = (grad * up * (s * (1.0 + gate * (1.0 - s)))).astype(BF)
            self.back[2, r, cs] = (grad * a).astype(BF)
        b = self.back.at[:, r, :]
        self.send(("s4", k), b, b, self.dev(c=1 - self.c))

    def J(self, k):
        self.wait(("s4", k), self.back.at[:, self.side(k, 1 - self.c), :], self.dev(c=1 - self.c))
        r = self.rows(k)
        self.tot[k] = jnp.dot(self.back[1, r, :], self.wg[...], preferred_element_type=F32) + jnp.dot(
            self.back[2, r, :], self.wu[...], preferred_element_type=F32
        )
        if k in YF:
            i = YF.index(k)
            for b in range(NX):
                self.by4[i, b * SH : (b + 1) * SH] = self.tot[k, self.strip(b, 1 - self.yl), :].astype(BF)
            self.send(("ry", k), self.by4.at[i], self.ry4.at[i], self.dev(yl=1 - self.yl))
        else:
            self.over_x(k)

    def strip(self, b, y):
        return pl.ds(pl.multiple_of(b * PAIR + y * SH, SH), SH)

    def Y(self, k):
        i = YF.index(k)
        self.wait(("ry", k), self.ry4.at[i], self.dev(yl=1 - self.yl))
        for b in range(NX):
            r = self.strip(b, self.yl)
            self.tot[k, r, :] = self.tot[k, r, :] + self.ry4[i, b * SH : (b + 1) * SH].astype(F32)
        self.over_x(k)

    def block(self, k, dx):
        if k in YF:
            return self.strip(self.xblock(dx), self.yl)
        return pl.ds(pl.multiple_of(self.xblock(dx) * PAIR, PAIR), PAIR)

    def over_x(self, k):
        n = pl.ds(0, SH if k in YF else PAIR)
        self.b1[k, n] = self.tot[k, self.block(k, 2), :].astype(BF)
        if k in DIRECT:
            self.send(("r1", k), self.b1.at[k, n], self.r1.at[k, n], self.dev(dx=2))
            for q in (0, 1):
                self.b2[k, q, n] = self.tot[k, self.block(k, 1 if q == 0 else -1), :].astype(BF)
                self.send(("r2", k, q), self.b2.at[k, q, n], self.r2.at[k, q, n], self.xd(q))
        else:
            for q in (0, 1):
                self.send(("r1", k, q), self.b1.at[k, n, self.half[q]], self.r1.at[k, n, self.half[q]], self.xd(q))

    def K(self, k):
        n = pl.ds(0, SH if k in YF else PAIR)
        for q in (0, 1):
            h, o = self.half[q], self.half[1 - q]
            self.wait(("r1", k, q), self.r1.at[k, n, h], self.xd(1 - q))
            b = self.block(k, 1 if q == 0 else -1)
            self.b2[k, q, n, h] = (self.tot[k, b, h] + self.r1[k, n, h].astype(F32)).astype(BF)
            self.b2[k, q, n, o] = self.tot[k, b, o].astype(BF)
            self.send(("r2", k, q), self.b2.at[k, q, n], self.r2.at[k, q, n], self.xd(q))

    def L(self, k):
        n = pl.ds(0, SH if k in YF else PAIR)
        for q in (0, 1):
            self.wait(("r2", k, q), self.r2.at[k, q, n], self.xd(1 - q))
        b = self.block(k, 0)
        s = self.tot[k, b, :] + self.r2[k, 0, n].astype(F32) + self.r2[k, 1, n].astype(F32)
        if k in DIRECT:
            self.wait(("r1", k), self.r1.at[k, n], self.dev(dx=2))
            s = s + self.r1[k, n].astype(F32)
        if k in YF:
            self.over_z(k, s)
            return
        self.tot[k, b, :] = s
        if k in FAR:
            for i, y in ((0, self.yl), (1, 1 - self.yl)):
                self.bz[k, i] = self.tot[k, self.yrows(y), :].astype(BF)
                self.send(("rz", k, i), self.bz.at[k, i], self.rz.at[k, i], self.dev(dz=offset(k), yl=y))
        else:
            self.by[k] = self.tot[k, self.yrows(1 - self.yl), :].astype(BF)
            self.send(("ry", k), self.by.at[k], self.ry.at[k], self.dev(yl=1 - self.yl))

    def yrows(self, y):
        return self.strip(self.xblock(0), y)

    def over_z(self, k, s):
        if k == 0:
            self.tot[k, self.yrows(self.yl), :] = s
        else:
            self.bz[k, 0] = s.astype(BF)
            self.send(("rz", k, 0), self.bz.at[k, 0], self.rz.at[k, 0], self.dev(dz=offset(k)))

    def M(self, k):
        self.wait(("ry", k), self.ry.at[k], self.dev(yl=1 - self.yl))
        self.over_z(k, self.tot[k, self.yrows(self.yl), :] + self.ry[k].astype(F32))

    def N(self):
        s = self.tot[0, self.yrows(self.yl), :]
        for k in range(1, NZ):
            for i, y in ((0, self.yl), (1, 1 - self.yl))[: 2 if k in FAR and k not in YF else 1]:
                self.wait(("rz", k, i), self.rz.at[k, i], self.dev(dz=-offset(k), yl=y))
                s = s + self.rz[k, i].astype(F32)
        self.out[...] = s.astype(BF)

    def turn(self):
        for i in range(3):
            self.ht[i] = self.back[i].T

    def W(self, j):
        n = self.tok.shape[1] // TILES
        cs = pl.ds(j * n, n)
        for i, a, o in ((1, self.tok, self.og), (2, self.tok, self.ou), (0, self.cot, self.od)):
            o[:, cs] = jnp.dot(self.ht[i], a[:, cs], preferred_element_type=F32).astype(BF)

    def finish(self):
        self.ready()
        for cp in self.sent:
            cp.wait_send()


NAMES = {"z": "zin", "x": "xin", "ht": "turn"}


def kernel(*refs):
    step = Step(refs)
    step.begin()
    for name, *args in ORDER:
        getattr(step, NAMES.get(name, name))(*args)
    step.finish()


def shards(tokens, grad_output, gate_weight, up_weight, down_weight):
    d, f = gate_weight.shape
    n = NZ * CHUNK
    anywhere = pl.BlockSpec(memory_space=pl.ANY)
    vmem = pltpu.VMEM
    grad_tokens, grad_gate, grad_up, grad_down = pl.pallas_call(
        kernel,
        out_shape=(
            vmem((SH, d), BF),
            vmem((f, d), BF),
            vmem((f, d), BF),
            vmem((f, d), BF),
        ),
        in_specs=[anywhere] * 5,
        out_specs=(pl.BlockSpec(memory_space=vmem),) * 4,
        scratch_shapes=[
            vmem((n, d), BF), vmem((n, d), BF),
            vmem((f, d), BF), vmem((f, d), BF), vmem((f, d), BF),
            vmem((NZ, 3, CHUNK, f), F32), vmem((NZ, 3, 64, f), F32), vmem((NZ, 672, 128), BF), vmem((NZ, 672, 128), BF),
            vmem((3, n, f), BF),
            vmem((NZ, CHUNK, d), F32),
            vmem((NZ, PAIR, d), BF), vmem((NZ, 2, PAIR, d), BF),
            vmem((NZ, PAIR, d), BF), vmem((NZ, 2, PAIR, d), BF),
            vmem((NZ, SH, d), BF), vmem((NZ, SH, d), BF), vmem((NZ, 2, SH, d), BF), vmem((NZ, 2, SH, d), BF),
            vmem((max(1, len(YF)), NX * SH, d), BF), vmem((max(1, len(YF)), NX * SH, d), BF),
            vmem((3, f, n), BF),
            pltpu.SemaphoreType.DMA((200,)), pltpu.SemaphoreType.DMA((200,)), pltpu.SemaphoreType.DMA((5,)),
        ],
        compiler_params=pltpu.CompilerParams(collective_id=0, has_side_effects=True, vmem_limit_bytes=57 << 20),
        cost_estimate=pl.CostEstimate(flops=16 * n * d * f, bytes_accessed=12 * d * f, transcendentals=n * f),
    )(tokens, grad_output, gate_weight.T, up_weight.T, down_weight)
    return grad_tokens, grad_gate.T, grad_up.T, grad_down


def solution(mesh):
    placed = (P("hid", "mod"), P("hid", "mod"), P("mod", "hid"), P("mod", "hid"), P("hid", "mod"))
    return jax.shard_map(
        shards,
        mesh=mesh,
        in_specs=placed,
        out_specs=(P("hid", "mod"), P("mod", "hid"), P("mod", "hid"), P("hid", "mod")),
        check_vma=False,
    )
```

```python
import functools

import jax
import jax.numpy as jnp
from jax import lax
from jax.experimental import pallas as pl
from jax.experimental.pallas import tpu as pltpu
from jax.sharding import PartitionSpec as P

MESH = pl.DeviceIdType.MESH
BF = jnp.bfloat16
F32 = jnp.float32
NT = (((1,), (1,)), ((), ()))

NX, NZ = 4, 8
SH = 16
PAIR = 2 * SH
CHUNK = NX * PAIR
TILES = 8
ZC = (7,)
TX = (1, 2, 3, 6)
YC = (1, 7)
YF = (2, 6)
DIRECT = (6, 7)
FAR = (5, 6)

ORDER = (
    ('own',), ('y',), ('x0', 'T', 0), ('x0', 'T', 1), ('z', 1, 'C'), ('z', 2, 'C'), ('cx', 2), ('cx', 1),
    ('x0', 'C', 0), ('x0', 'C', 1), ('z', 1, 'T0'), ('z', 2, 'T0'), ('x0b', 'T'), ('A', 0), ('z', 1, 'T1'),
    ('z', 2, 'T1'), ('x', 2, 0), ('x', 2, 1), ('z', 1, 'T2'), ('z', 2, 'T2'), ('x', 1, 0), ('x', 1, 1), ('x0b', 'C'),
    ('F', 0), ('z', 3, 'C'), ('z', 4, 'C'), ('cx', 3), ('cx', 4), ('G', 0), ('t3', 1), ('A', 1), ('z', 3, 'T0'),
    ('z', 4, 'T0'), ('xb', 2), ('t3', 2), ('A', 2), ('F', 2), ('xb', 1), ('z', 3, 'T1'), ('z', 4, 'T1'), ('G', 2),
    ('x', 3, 0), ('x', 3, 1), ('H', 0), ('yc', 1), ('z', 3, 'T2'), ('z', 4, 'T2'), ('F', 1), ('J', 0), ('G', 1),
    ('z', 5, 'C'), ('z', 6, 'C'), ('cx', 5), ('x', 4, 0), ('x', 4, 1), ('xb', 3), ('cx', 6), ('t3', 3), ('A', 3),
    ('F', 3), ('H', 2), ('z', 5, 'T0'), ('z', 6, 'T0'), ('K', 0), ('G', 3), ('J', 2), ('z', 4, 'T3'), ('z', 5, 'T1'),
    ('A', 4), ('H', 1), ('x', 5, 0), ('x', 5, 1), ('xb', 4), ('F', 4), ('z', 5, 'T2'), ('z', 6, 'T1'), ('J', 1),
    ('H', 3), ('z', 6, 'T2'), ('x', 6, 0), ('x', 6, 1), ('G', 4), ('J', 3), ('z', 5, 'T3'), ('z', 7, 'C'),
    ('z', 7, 'T0'), ('xb', 5), ('A', 5), ('F', 5), ('z', 7, 'T1'), ('Y', 2), ('L', 0), ('K', 1), ('t3', 6), ('G', 5),
    ('A', 6), ('z', 7, 'C1'), ('xb', 6), ('F', 6), ('H', 4), ('z', 7, 'T2'), ('z', 7, 'C2'), ('K', 3), ('K', 2),
    ('G', 6), ('z', 7, 'T3'), ('A', 7), ('M', 0), ('z', 7, 'C3'), ('F', 7), ('J', 4), ('H', 5), ('G', 7), ('L', 1),
    ('L', 3), ('J', 5), ('L', 2), ('H', 6), ('K', 4), ('J', 6), ('K', 5), ('H', 7), ('M', 1), ('J', 7), ('M', 3),
    ('L', 4), ('ht',), ('W', 0), ('L', 5), ('W', 1), ('W', 2), ('Y', 6), ('W', 3), ('L', 7), ('M', 4), ('W', 4),
    ('W', 5), ('L', 6), ('M', 7), ('W', 6), ('W', 7), ('N',),
)


def distance(k):
    return (k + 1) // 2


def offset(k):
    return distance(k) if k % 2 == 0 else -distance(k)


class Step:
    def __init__(self, refs):
        (self.tok_in, self.cot_in, self.wg_in, self.wu_in, self.wd_in,
         self.out, self.og, self.ou, self.od,
         self.tok, self.cot, self.wg, self.wu, self.wd, self.part, self.s1, self.g2, self.s2, self.back,
         self.tot, self.b1, self.b2, self.r1, self.r2, self.by, self.ry, self.bz, self.rz, self.by4, self.ry4,
         self.ht, self.send_sem, self.recv_sem, self.local_sem) = refs
        hid, mod = lax.axis_index("hid"), lax.axis_index("mod")
        self.x, self.yl, self.z = hid // 16, (hid // 8) % 2, hid % 8
        self.yh, self.c = mod // 2, mod % 2
        self.ids = {}
        self.sent = []
        self.n_local = 0
        half = self.tok.shape[1] // 2
        self.half = (pl.ds(0, half), pl.ds(half, half))

    def dev(self, dx=0, dz=0, yl=None, yh=None, c=None):
        x = lax.rem(self.x + (dx + NX), NX)
        z = lax.rem(self.z + (dz + NZ), NZ)
        yl = self.yl if yl is None else yl
        yh = self.yh if yh is None else yh
        c = self.c if c is None else c
        return (x * 16 + yl * 8 + z, yh * 2 + c)

    def zchunk(self, k):
        return lax.rem(self.z + (offset(k) + NZ), NZ)

    def xblock(self, dx):
        return lax.rem(self.x + (dx + NX), NX)

    def rows(self, k, dx=None, y=None):
        base = self.zchunk(k) * CHUNK
        if dx is None:
            return pl.ds(pl.multiple_of(base, CHUNK), CHUNK)
        base = base + self.xblock(dx) * PAIR
        if y is None:
            return pl.ds(pl.multiple_of(base, PAIR), PAIR)
        return pl.ds(pl.multiple_of(base + y * SH, SH), SH)

    def side(self, k, c):
        return pl.ds(pl.multiple_of(self.zchunk(k) * CHUNK + c * 64, 64), 64)

    def sem(self, key):
        return self.ids.setdefault(key, len(self.ids))

    def send(self, key, src, dst, dev):
        i = self.sem(key)
        cp = pltpu.make_async_remote_copy(src_ref=src, dst_ref=dst, send_sem=self.send_sem.at[i],
                                          recv_sem=self.recv_sem.at[i], device_id=dev, device_id_type=MESH)
        cp.start()
        self.sent.append(cp)

    def wait(self, key, dst, dev):
        i = self.sem(key)
        pltpu.make_async_remote_copy(src_ref=dst, dst_ref=dst, send_sem=self.send_sem.at[i],
                                     recv_sem=self.recv_sem.at[i], device_id=dev, device_id_type=MESH).wait_recv()

    def fetch(self, src, dst):
        cp = pltpu.make_async_copy(src, dst, self.local_sem.at[self.n_local])
        self.n_local += 1
        cp.start()
        return cp

    def xd(self, q):
        return self.dev(dx=1 if q == 0 else -1)

    def zd(self, q):
        return self.dev(dz=1 if q == 0 else -1)

    def arr(self, a):
        return self.tok if a == "T" else self.cot

    def begin(self):
        own = self.rows(0, 0, self.yl)
        first = (self.fetch(self.tok_in, self.tok.at[own]), self.fetch(self.cot_in, self.cot.at[own]))
        self.weights = (self.fetch(self.wg_in, self.wg), self.fetch(self.wu_in, self.wu), self.fetch(self.wd_in, self.wd))
        bar = pltpu.get_barrier_semaphore()
        peers = [self.xd(0), self.xd(1), self.dev(yl=1 - self.yl), self.dev(yh=1 - self.yh), self.dev(c=1 - self.c)]
        peers += [self.zd(0), self.zd(1)]
        for p in peers:
            pl.semaphore_signal(bar, inc=1, device_id=p, device_id_type=MESH)
        pl.semaphore_wait(bar, len(peers))
        for cp in first:
            cp.wait()

    def plane(self, to, a, y, part):
        r = self.arr(a).at[self.rows(0, 0, y)]
        for q in (0, 1):
            if to == "x":
                self.send(("x0", a, q, part), r, r, self.xd(q))
            else:
                self.send(("z", 1 + q, a + "o", part), r, r, self.zd(q))

    def own(self):
        for a in "TC":
            r = self.arr(a).at[self.rows(0, 0, self.yl)]
            self.send(("y", a), r, r, self.dev(yl=1 - self.yl))
        for to, a in (("x", "T"), ("x", "C"), ("z", "C"), ("z", "T")):
            self.plane(to, a, self.yl, 0)

    def y(self):
        for a in "TC":
            self.wait(("y", a), self.arr(a).at[self.rows(0, 0, 1 - self.yl)], self.dev(yl=1 - self.yl))
        for to, a in (("x", "T"), ("x", "C"), ("z", "C"), ("z", "T")):
            if (to, a) != ("x", "C") or 0 not in YC:
                self.plane(to, a, 1 - self.yl, 1)

    def x0(self, a, q):
        dx = -1 if q == 0 else 1
        ys = (self.yl, 1 - self.yl)
        if a == "C" and 0 in YC:
            ys = ys[:1]
        for part, y in enumerate(ys):
            self.wait(("x0", a, q, part), self.arr(a).at[self.rows(0, dx, y)], self.xd(1 - q))
        rows = self.crows(0, dx) if a == "C" else self.rows(0, dx)
        r = self.arr(a).at[rows]
        h = self.arr(a).at[rows, self.half[q]]
        self.send(("x0b", a, q), h, h, self.xd(q))
        if a == "T":
            for p in (0, 1):
                self.send(("z", 1 + p, "T%d" % (1 + q), 0), r, r, self.zd(p))
        else:
            self.gathered(0, q, dx, r)

    def x0b(self, a):
        rows = self.crows(0, 2) if a == "C" else self.rows(0, 2)
        for q in (0, 1):
            self.wait(("x0b", a, q), self.arr(a).at[rows, self.half[q]], self.xd(1 - q))
        r = self.arr(a).at[rows]
        if a == "T":
            for p in (0, 1):
                if 1 + p not in TX:
                    self.send(("z", 1 + p, "T3", 0), r, r, self.zd(p))
        else:
            self.gathered(0, 2, 2, r)

    def zin(self, k, p):
        d = 0 if k % 2 else 1
        a = self.arr(p[0])
        dx = {"": 0, "0": 0, "1": -1, "2": 1, "3": 2}[p[1:]]
        r = a.at[self.rows(k, dx)]
        if k == 7:
            for q in (0, 1):
                self.wait(("z", 7, p, q), a.at[self.rows(k, dx), self.half[q]], self.zd(1 - q))
        elif k <= 2 and dx == 0:
            for part, y in ((0, self.yl), (1, 1 - self.yl)):
                self.wait(("z", k, p[0] + "o", part), a.at[self.rows(k, dx, y)], self.zd(1 - d))
        else:
            self.wait(("z", k, p, 0), r, self.zd(1 - d))
        if p != "T3" or min(k + 2, 7) not in TX:
            self.onward(k, p, dx)
        if k in TX and p in ("T1", "T2"):
            q = 0 if p == "T1" else 1
            h = a.at[self.rows(k, dx), self.half[q]]
            self.send(("t3", k, q), h, h, self.xd(q))

    def onward(self, k, p, dx):
        d = 0 if k % 2 else 1
        a = self.arr(p[0])
        if k < 5:
            r = a.at[self.rows(k, dx)]
            self.send(("z", k + 2, p, 0), r, r, self.zd(d))
        elif k < 7:
            h = a.at[self.rows(k, dx), self.half[d]]
            self.send(("z", 7, p, d), h, h, self.zd(d))

    def t3(self, k):
        for q in (0, 1):
            self.wait(("t3", k, q), self.tok.at[self.rows(k, 2), self.half[q]], self.xd(1 - q))
        if min(k + 2, 7) not in TX:
            self.onward(k, "T3", 2)

    def crows(self, k, dx):
        return self.rows(k, dx, self.yl if k in YC else None)

    def cx(self, k):
        r = self.cot.at[self.crows(k, 0)]
        for q in (0, 1):
            self.send(("x", k, q), r, r, self.xd(q))

    def xin(self, k, q):
        dx = -1 if q == 0 else 1
        r = self.cot.at[self.crows(k, dx)]
        self.wait(("x", k, q), r, self.xd(1 - q))
        h = self.cot.at[self.crows(k, dx), self.half[q]]
        self.send(("xb", k, q), h, h, self.xd(q))
        self.gathered(k, q, dx, r)

    def xb(self, k):
        for q in (0, 1):
            self.wait(("xb", k, q), self.cot.at[self.crows(k, 2), self.half[q]], self.xd(1 - q))
        self.gathered(k, 2, 2, self.cot.at[self.crows(k, 2)])

    def gathered(self, k, i, dx, r):
        if k in YC:
            self.send(("yc", k, i), r, r, self.dev(yl=1 - self.yl))
        elif k and min(k + 2, 7) in ZC:
            self.onward(k, "C%d" % (1 + i), dx)

    def yc(self, k):
        for i, dx in enumerate((-1, 1, 2)):
            self.wait(("yc", k, i), self.cot.at[self.rows(k, dx, 1 - self.yl)], self.dev(yl=1 - self.yl))
        if k and min(k + 2, 7) in ZC:
            for i, dx in enumerate((-1, 1, 2)):
                self.onward(k, "C%d" % (1 + i), dx)

    def ready(self):
        for cp in self.weights:
            cp.wait()
        self.weights = ()

    def A(self, k):
        self.ready()
        r = self.rows(k)
        t = self.tok[r, :]
        self.part[k, 0] = lax.dot_general(t, self.wg[...], NT, preferred_element_type=F32)
        self.part[k, 1] = lax.dot_general(t, self.wu[...], NT, preferred_element_type=F32)

    def F(self, k):
        r = self.rows(k)
        self.part[k, 2] = lax.dot_general(self.cot[r, :], self.wd[...], NT, preferred_element_type=F32)
        other = pl.ds(pl.multiple_of((1 - self.c) * 64, 64), 64)
        self.send(("s1", k), self.part.at[k, :, other, :], self.s1.at[k], self.dev(c=1 - self.c))

    def G(self, k):
        self.wait(("s1", k), self.s1.at[k], self.dev(c=1 - self.c))
        mine = pl.ds(pl.multiple_of(self.c * 64, 64), 64)
        rest = []
        for i in range(3):
            total = self.part[k, i, mine, :] + self.s1[k, i]
            self.s1[k, i] = total
            low = total.astype(BF)
            for t in range(3):
                self.g2[k, (i * 3 + t) * 64 : (i * 3 + t + 1) * 64, :] = low[:, t * 128 : (t + 1) * 128]
            rest.append(low[:, 384:])
        self.g2[k, 576:640, :] = jnp.concatenate(rest[:2], axis=1)
        self.g2[k, 640:, :] = jnp.concatenate([rest[2][:32], rest[2][32:]], axis=1)
        self.send(("s2", k), self.g2.at[k], self.s2.at[k], self.dev(yh=1 - self.yh))

    def H(self, k):
        self.wait(("s2", k), self.s2.at[k], self.dev(yh=1 - self.yh))
        r = self.side(k, self.c)
        pair, last = self.s2[k, 576:640, :], self.s2[k, 640:, :]
        rest = (pair[:, :64], pair[:, 64:], jnp.concatenate([last[:, :64], last[:, 64:]], axis=0))
        for t in range(4):
            cs = pl.ds(t * 128, 128 if t < 3 else 64)
            far = [self.s2[k, (i * 3 + t) * 64 : (i * 3 + t + 1) * 64, :] if t < 3 else rest[i] for i in range(3)]
            gate, up, grad = (self.s1[k, i, :, cs] + far[i].astype(F32) for i in range(3))
            s = jax.nn.sigmoid(gate)
            a = gate * s
            self.back[0, r, cs] = (a * up).astype(BF)
            self.back[1, r, cs] = (grad * up * (s * (1.0 + gate * (1.0 - s)))).astype(BF)
            self.back[2, r, cs] = (grad * a).astype(BF)
        b = self.back.at[:, r, :]
        self.send(("s4", k), b, b, self.dev(c=1 - self.c))

    def J(self, k):
        self.wait(("s4", k), self.back.at[:, self.side(k, 1 - self.c), :], self.dev(c=1 - self.c))
        r = self.rows(k)
        self.tot[k] = jnp.dot(self.back[1, r, :], self.wg[...], preferred_element_type=F32) + jnp.dot(
            self.back[2, r, :], self.wu[...], preferred_element_type=F32
        )
        if k in YF:
            i = YF.index(k)
            for b in range(NX):
                self.by4[i, b * SH : (b + 1) * SH] = self.tot[k, self.strip(b, 1 - self.yl), :].astype(BF)
            self.send(("ry", k), self.by4.at[i], self.ry4.at[i], self.dev(yl=1 - self.yl))
        else:
            self.over_x(k)

    def strip(self, b, y):
        return pl.ds(pl.multiple_of(b * PAIR + y * SH, SH), SH)

    def Y(self, k):
        i = YF.index(k)
        self.wait(("ry", k), self.ry4.at[i], self.dev(yl=1 - self.yl))
        for b in range(NX):
            r = self.strip(b, self.yl)
            self.tot[k, r, :] = self.tot[k, r, :] + self.ry4[i, b * SH : (b + 1) * SH].astype(F32)
        self.over_x(k)

    def block(self, k, dx):
        if k in YF:
            return self.strip(self.xblock(dx), self.yl)
        return pl.ds(pl.multiple_of(self.xblock(dx) * PAIR, PAIR), PAIR)

    def over_x(self, k):
        n = pl.ds(0, SH if k in YF else PAIR)
        self.b1[k, n] = self.tot[k, self.block(k, 2), :].astype(BF)
        if k in DIRECT:
            self.send(("r1", k), self.b1.at[k, n], self.r1.at[k, n], self.dev(dx=2))
            for q in (0, 1):
                self.b2[k, q, n] = self.tot[k, self.block(k, 1 if q == 0 else -1), :].astype(BF)
                self.send(("r2", k, q), self.b2.at[k, q, n], self.r2.at[k, q, n], self.xd(q))
        else:
            for q in (0, 1):
                self.send(("r1", k, q), self.b1.at[k, n, self.half[q]], self.r1.at[k, n, self.half[q]], self.xd(q))

    def K(self, k):
        n = pl.ds(0, SH if k in YF else PAIR)
        for q in (0, 1):
            h, o = self.half[q], self.half[1 - q]
            self.wait(("r1", k, q), self.r1.at[k, n, h], self.xd(1 - q))
            b = self.block(k, 1 if q == 0 else -1)
            self.b2[k, q, n, h] = (self.tot[k, b, h] + self.r1[k, n, h].astype(F32)).astype(BF)
            self.b2[k, q, n, o] = self.tot[k, b, o].astype(BF)
            self.send(("r2", k, q), self.b2.at[k, q, n], self.r2.at[k, q, n], self.xd(q))

    def L(self, k):
        n = pl.ds(0, SH if k in YF else PAIR)
        for q in (0, 1):
            self.wait(("r2", k, q), self.r2.at[k, q, n], self.xd(1 - q))
        b = self.block(k, 0)
        s = self.tot[k, b, :] + self.r2[k, 0, n].astype(F32) + self.r2[k, 1, n].astype(F32)
        if k in DIRECT:
            self.wait(("r1", k), self.r1.at[k, n], self.dev(dx=2))
            s = s + self.r1[k, n].astype(F32)
        if k in YF:
            self.over_z(k, s)
            return
        self.tot[k, b, :] = s
        if k in FAR:
            for i, y in ((0, self.yl), (1, 1 - self.yl)):
                self.bz[k, i] = self.tot[k, self.yrows(y), :].astype(BF)
                self.send(("rz", k, i), self.bz.at[k, i], self.rz.at[k, i], self.dev(dz=offset(k), yl=y))
        else:
            self.by[k] = self.tot[k, self.yrows(1 - self.yl), :].astype(BF)
            self.send(("ry", k), self.by.at[k], self.ry.at[k], self.dev(yl=1 - self.yl))

    def yrows(self, y):
        return self.strip(self.xblock(0), y)

    def over_z(self, k, s):
        if k == 0:
            self.tot[k, self.yrows(self.yl), :] = s
        else:
            self.bz[k, 0] = s.astype(BF)
            self.send(("rz", k, 0), self.bz.at[k, 0], self.rz.at[k, 0], self.dev(dz=offset(k)))

    def M(self, k):
        self.wait(("ry", k), self.ry.at[k], self.dev(yl=1 - self.yl))
        self.over_z(k, self.tot[k, self.yrows(self.yl), :] + self.ry[k].astype(F32))

    def N(self):
        s = self.tot[0, self.yrows(self.yl), :]
        for k in range(1, NZ):
            for i, y in ((0, self.yl), (1, 1 - self.yl))[: 2 if k in FAR and k not in YF else 1]:
                self.wait(("rz", k, i), self.rz.at[k, i], self.dev(dz=-offset(k), yl=y))
                s = s + self.rz[k, i].astype(F32)
        self.out[...] = s.astype(BF)

    def turn(self):
        for i in range(3):
            self.ht[i] = self.back[i].T

    def W(self, j):
        n = self.tok.shape[1] // TILES
        cs = pl.ds(j * n, n)
        for i, a, o in ((1, self.tok, self.og), (2, self.tok, self.ou), (0, self.cot, self.od)):
            o[:, cs] = jnp.dot(self.ht[i], a[:, cs], preferred_element_type=F32).astype(BF)

    def finish(self):
        self.ready()
        for cp in self.sent:
            cp.wait_send()


NAMES = {"z": "zin", "x": "xin", "ht": "turn"}


def kernel(*refs):
    step = Step(refs)
    step.begin()
    for name, *args in ORDER:
        getattr(step, NAMES.get(name, name))(*args)
    step.finish()


def hand_over(*refs):
    *arrays, sem = refs
    copies = [pltpu.make_async_copy(arrays[i], arrays[4 + i], sem.at[i]) for i in range(4)]
    for cp in copies:
        cp.start()
    for cp in copies:
        cp.wait()


def shards(tokens, grad_output, gate_weight, up_weight, down_weight):
    d, f = gate_weight.shape
    n = NZ * CHUNK
    anywhere = pl.BlockSpec(memory_space=pl.ANY)
    vmem = pltpu.VMEM
    results = pl.pallas_call(
        kernel,
        out_shape=(
            vmem((SH, d), BF),
            vmem((f, d), BF),
            vmem((f, d), BF),
            vmem((f, d), BF),
        ),
        in_specs=[anywhere] * 5,
        out_specs=(pl.BlockSpec(memory_space=vmem),) * 4,
        scratch_shapes=[
            vmem((n, d), BF), vmem((n, d), BF),
            vmem((f, d), BF), vmem((f, d), BF), vmem((f, d), BF),
            vmem((NZ, 3, CHUNK, f), F32), vmem((NZ, 3, 64, f), F32), vmem((NZ, 672, 128), BF), vmem((NZ, 672, 128), BF),
            vmem((3, n, f), BF),
            vmem((NZ, CHUNK, d), F32),
            vmem((NZ, PAIR, d), BF), vmem((NZ, 2, PAIR, d), BF),
            vmem((NZ, PAIR, d), BF), vmem((NZ, 2, PAIR, d), BF),
            vmem((NZ, SH, d), BF), vmem((NZ, SH, d), BF), vmem((NZ, 2, SH, d), BF), vmem((NZ, 2, SH, d), BF),
            vmem((max(1, len(YF)), NX * SH, d), BF), vmem((max(1, len(YF)), NX * SH, d), BF),
            vmem((3, f, n), BF),
            pltpu.SemaphoreType.DMA((200,)), pltpu.SemaphoreType.DMA((200,)), pltpu.SemaphoreType.DMA((5,)),
        ],
        compiler_params=pltpu.CompilerParams(collective_id=0, has_side_effects=True, vmem_limit_bytes=55 << 20),
        cost_estimate=pl.CostEstimate(flops=16 * n * d * f, bytes_accessed=12 * d * f, transcendentals=n * f),
    )(tokens, grad_output, gate_weight.T, up_weight.T, down_weight)
    grad_tokens, grad_gate, grad_up, grad_down = pl.pallas_call(
        hand_over,
        out_shape=tuple(jax.ShapeDtypeStruct(r.shape, r.dtype) for r in results),
        in_specs=[pl.BlockSpec(memory_space=vmem)] * 4,
        out_specs=(anywhere,) * 4,
        scratch_shapes=[pltpu.SemaphoreType.DMA((4,))],
        compiler_params=pltpu.CompilerParams(vmem_limit_bytes=1 << 20),
    )(*(pltpu.with_memory_space_constraint(r, vmem) for r in results))
    return grad_tokens, grad_gate.T, grad_up.T, grad_down


def solution(mesh):
    placed = (P("hid", "mod"), P("hid", "mod"), P("mod", "hid"), P("mod", "hid"), P("hid", "mod"))
    return jax.shard_map(
        shards,
        mesh=mesh,
        in_specs=placed,
        out_specs=(P("hid", "mod"), P("mod", "hid"), P("mod", "hid"), P("hid", "mod")),
        check_vma=False,
    )
```

```python
import functools

import jax
import jax.numpy as jnp
from jax import lax
from jax.experimental import pallas as pl
from jax.experimental.pallas import tpu as pltpu
from jax.sharding import PartitionSpec as P

MESH = pl.DeviceIdType.MESH
BF = jnp.bfloat16
F32 = jnp.float32
NT = (((1,), (1,)), ((), ()))

NX, NZ = 4, 8
SH = 16
PAIR = 2 * SH
CHUNK = NX * PAIR
TILES = 8
ZC = (7,)
TX = (1, 2, 3, 6)
YC = (1, 7)
YF = (2, 6)
DIRECT = (6, 7)
FAR = (5, 6)

ORDER = (
    ('own',), ('y',), ('x0', 'T', 0), ('x0', 'T', 1), ('z', 1, 'C'), ('z', 2, 'C'), ('cx', 2), ('cx', 1),
    ('x0', 'C', 0), ('x0', 'C', 1), ('z', 1, 'T0'), ('z', 2, 'T0'), ('x0b', 'T'), ('A', 0), ('z', 1, 'T1'),
    ('z', 2, 'T1'), ('x', 2, 0), ('x', 2, 1), ('z', 1, 'T2'), ('z', 2, 'T2'), ('x', 1, 0), ('x', 1, 1), ('x0b', 'C'),
    ('F', 0), ('z', 3, 'C'), ('z', 4, 'C'), ('cx', 3), ('cx', 4), ('G', 0), ('t3', 1), ('A', 1), ('z', 3, 'T0'),
    ('z', 4, 'T0'), ('xb', 2), ('t3', 2), ('A', 2), ('F', 2), ('xb', 1), ('z', 3, 'T1'), ('z', 4, 'T1'), ('G', 2),
    ('x', 3, 0), ('x', 3, 1), ('H', 0), ('yc', 1), ('z', 3, 'T2'), ('z', 4, 'T2'), ('F', 1), ('J', 0), ('G', 1),
    ('z', 5, 'C'), ('z', 6, 'C'), ('cx', 5), ('x', 4, 0), ('x', 4, 1), ('xb', 3), ('cx', 6), ('t3', 3), ('A', 3),
    ('F', 3), ('H', 2), ('z', 5, 'T0'), ('z', 6, 'T0'), ('K', 0), ('G', 3), ('J', 2), ('z', 4, 'T3'), ('z', 5, 'T1'),
    ('A', 4), ('H', 1), ('x', 5, 0), ('x', 5, 1), ('xb', 4), ('F', 4), ('z', 5, 'T2'), ('z', 6, 'T1'), ('J', 1),
    ('H', 3), ('z', 6, 'T2'), ('x', 6, 0), ('x', 6, 1), ('G', 4), ('J', 3), ('z', 5, 'T3'), ('z', 7, 'C'),
    ('z', 7, 'T0'), ('xb', 5), ('A', 5), ('F', 5), ('z', 7, 'T1'), ('Y', 2), ('L', 0), ('K', 1), ('t3', 6), ('G', 5),
    ('A', 6), ('z', 7, 'C1'), ('xb', 6), ('F', 6), ('H', 4), ('z', 7, 'T2'), ('z', 7, 'C2'), ('K', 3), ('K', 2),
    ('G', 6), ('z', 7, 'T3'), ('A', 7), ('M', 0), ('z', 7, 'C3'), ('F', 7), ('J', 4), ('H', 5), ('G', 7), ('L', 1),
    ('L', 3), ('J', 5), ('L', 2), ('H', 6), ('K', 4), ('J', 6), ('K', 5), ('H', 7), ('M', 1), ('J', 7), ('M', 3),
    ('L', 4), ('ht',), ('W', 0), ('L', 5), ('W', 1), ('W', 2), ('Y', 6), ('W', 3), ('L', 7), ('M', 4), ('W', 4),
    ('W', 5), ('L', 6), ('M', 7), ('W', 6), ('W', 7), ('N',),
)


def distance(k):
    return (k + 1) // 2


def offset(k):
    return distance(k) if k % 2 == 0 else -distance(k)


class Step:
    def __init__(self, refs):
        (self.tok_in, self.cot_in, self.wg_in, self.wu_in, self.wd_in,
         self.out, self.og, self.ou, self.od,
         self.tok, self.cot, self.wg, self.wu, self.wd, self.part, self.s1, self.g2, self.s2, self.back,
         self.tot, self.b1, self.b2, self.r1, self.r2, self.by, self.ry, self.bz, self.rz, self.by4, self.ry4,
         self.ht, self.send_sem, self.recv_sem, self.local_sem) = refs
        hid, mod = lax.axis_index("hid"), lax.axis_index("mod")
        self.x, self.yl, self.z = hid // 16, (hid // 8) % 2, hid % 8
        self.yh, self.c = mod // 2, mod % 2
        self.ids = {}
        self.sent = []
        self.n_local = 0
        half = self.tok.shape[1] // 2
        self.half = (pl.ds(0, half), pl.ds(half, half))

    def dev(self, dx=0, dz=0, yl=None, yh=None, c=None):
        x = lax.rem(self.x + (dx + NX), NX)
        z = lax.rem(self.z + (dz + NZ), NZ)
        yl = self.yl if yl is None else yl
        yh = self.yh if yh is None else yh
        c = self.c if c is None else c
        return (x * 16 + yl * 8 + z, yh * 2 + c)

    def zchunk(self, k):
        return lax.rem(self.z + (offset(k) + NZ), NZ)

    def xblock(self, dx):
        return lax.rem(self.x + (dx + NX), NX)

    def rows(self, k, dx=None, y=None):
        base = self.zchunk(k) * CHUNK
        if dx is None:
            return pl.ds(pl.multiple_of(base, CHUNK), CHUNK)
        base = base + self.xblock(dx) * PAIR
        if y is None:
            return pl.ds(pl.multiple_of(base, PAIR), PAIR)
        return pl.ds(pl.multiple_of(base + y * SH, SH), SH)

    def side(self, k, c):
        return pl.ds(pl.multiple_of(self.zchunk(k) * CHUNK + c * 64, 64), 64)

    def sem(self, key):
        return self.ids.setdefault(key, len(self.ids))

    def send(self, key, src, dst, dev):
        i = self.sem(key)
        cp = pltpu.make_async_remote_copy(src_ref=src, dst_ref=dst, send_sem=self.send_sem.at[i],
                                          recv_sem=self.recv_sem.at[i], device_id=dev, device_id_type=MESH)
        cp.start()
        self.sent.append(cp)

    def wait(self, key, dst, dev):
        i = self.sem(key)
        pltpu.make_async_remote_copy(src_ref=dst, dst_ref=dst, send_sem=self.send_sem.at[i],
                                     recv_sem=self.recv_sem.at[i], device_id=dev, device_id_type=MESH).wait_recv()

    def fetch(self, src, dst):
        cp = pltpu.make_async_copy(src, dst, self.local_sem.at[self.n_local])
        self.n_local += 1
        cp.start()
        return cp

    def xd(self, q):
        return self.dev(dx=1 if q == 0 else -1)

    def zd(self, q):
        return self.dev(dz=1 if q == 0 else -1)

    def arr(self, a):
        return self.tok if a == "T" else self.cot

    def begin(self):
        own = self.rows(0, 0, self.yl)
        first = (self.fetch(self.tok_in, self.tok.at[own]), self.fetch(self.cot_in, self.cot.at[own]))
        self.weights = (self.fetch(self.wg_in, self.wg), self.fetch(self.wu_in, self.wu), self.fetch(self.wd_in, self.wd))
        bar = pltpu.get_barrier_semaphore()
        peers = [self.xd(0), self.xd(1), self.dev(yl=1 - self.yl), self.dev(yh=1 - self.yh), self.dev(c=1 - self.c)]
        peers += [self.zd(0), self.zd(1)]
        for p in peers:
            pl.semaphore_signal(bar, inc=1, device_id=p, device_id_type=MESH)
        pl.semaphore_wait(bar, len(peers))
        for cp in first:
            cp.wait()

    def plane(self, to, a, y, part):
        r = self.arr(a).at[self.rows(0, 0, y)]
        for q in (0, 1):
            if to == "x":
                self.send(("x0", a, q, part), r, r, self.xd(q))
            else:
                self.send(("z", 1 + q, a + "o", part), r, r, self.zd(q))

    def own(self):
        for a in "TC":
            r = self.arr(a).at[self.rows(0, 0, self.yl)]
            self.send(("y", a), r, r, self.dev(yl=1 - self.yl))
        for to, a in (("x", "T"), ("x", "C"), ("z", "C"), ("z", "T")):
            self.plane(to, a, self.yl, 0)

    def y(self):
        for a in "TC":
            self.wait(("y", a), self.arr(a).at[self.rows(0, 0, 1 - self.yl)], self.dev(yl=1 - self.yl))
        for to, a in (("x", "T"), ("x", "C"), ("z", "C"), ("z", "T")):
            if (to, a) != ("x", "C") or 0 not in YC:
                self.plane(to, a, 1 - self.yl, 1)

    def x0(self, a, q):
        dx = -1 if q == 0 else 1
        ys = (self.yl, 1 - self.yl)
        if a == "C" and 0 in YC:
            ys = ys[:1]
        for part, y in enumerate(ys):
            self.wait(("x0", a, q, part), self.arr(a).at[self.rows(0, dx, y)], self.xd(1 - q))
        rows = self.crows(0, dx) if a == "C" else self.rows(0, dx)
        r = self.arr(a).at[rows]
        h = self.arr(a).at[rows, self.half[q]]
        self.send(("x0b", a, q), h, h, self.xd(q))
        if a == "T":
            for p in (0, 1):
                self.send(("z", 1 + p, "T%d" % (1 + q), 0), r, r, self.zd(p))
        else:
            self.gathered(0, q, dx, r)

    def x0b(self, a):
        rows = self.crows(0, 2) if a == "C" else self.rows(0, 2)
        for q in (0, 1):
            self.wait(("x0b", a, q), self.arr(a).at[rows, self.half[q]], self.xd(1 - q))
        r = self.arr(a).at[rows]
        if a == "T":
            for p in (0, 1):
                if 1 + p not in TX:
                    self.send(("z", 1 + p, "T3", 0), r, r, self.zd(p))
        else:
            self.gathered(0, 2, 2, r)

    def zin(self, k, p):
        d = 0 if k % 2 else 1
        a = self.arr(p[0])
        dx = {"": 0, "0": 0, "1": -1, "2": 1, "3": 2}[p[1:]]
        r = a.at[self.rows(k, dx)]
        if k == 7:
            for q in (0, 1):
                self.wait(("z", 7, p, q), a.at[self.rows(k, dx), self.half[q]], self.zd(1 - q))
        elif k <= 2 and dx == 0:
            for part, y in ((0, self.yl), (1, 1 - self.yl)):
                self.wait(("z", k, p[0] + "o", part), a.at[self.rows(k, dx, y)], self.zd(1 - d))
        else:
            self.wait(("z", k, p, 0), r, self.zd(1 - d))
        if p != "T3" or min(k + 2, 7) not in TX:
            self.onward(k, p, dx)
        if k in TX and p in ("T1", "T2"):
            q = 0 if p == "T1" else 1
            h = a.at[self.rows(k, dx), self.half[q]]
            self.send(("t3", k, q), h, h, self.xd(q))

    def onward(self, k, p, dx):
        d = 0 if k % 2 else 1
        a = self.arr(p[0])
        if k < 5:
            r = a.at[self.rows(k, dx)]
            self.send(("z", k + 2, p, 0), r, r, self.zd(d))
        elif k < 7:
            h = a.at[self.rows(k, dx), self.half[d]]
            self.send(("z", 7, p, d), h, h, self.zd(d))

    def t3(self, k):
        for q in (0, 1):
            self.wait(("t3", k, q), self.tok.at[self.rows(k, 2), self.half[q]], self.xd(1 - q))
        if min(k + 2, 7) not in TX:
            self.onward(k, "T3", 2)

    def crows(self, k, dx):
        return self.rows(k, dx, self.yl if k in YC else None)

    def cx(self, k):
        r = self.cot.at[self.crows(k, 0)]
        for q in (0, 1):
            self.send(("x", k, q), r, r, self.xd(q))

    def xin(self, k, q):
        dx = -1 if q == 0 else 1
        r = self.cot.at[self.crows(k, dx)]
        self.wait(("x", k, q), r, self.xd(1 - q))
        h = self.cot.at[self.crows(k, dx), self.half[q]]
        self.send(("xb", k, q), h, h, self.xd(q))
        self.gathered(k, q, dx, r)

    def xb(self, k):
        for q in (0, 1):
            self.wait(("xb", k, q), self.cot.at[self.crows(k, 2), self.half[q]], self.xd(1 - q))
        self.gathered(k, 2, 2, self.cot.at[self.crows(k, 2)])

    def gathered(self, k, i, dx, r):
        if k in YC:
            self.send(("yc", k, i), r, r, self.dev(yl=1 - self.yl))
        elif k and min(k + 2, 7) in ZC:
            self.onward(k, "C%d" % (1 + i), dx)

    def yc(self, k):
        for i, dx in enumerate((-1, 1, 2)):
            self.wait(("yc", k, i), self.cot.at[self.rows(k, dx, 1 - self.yl)], self.dev(yl=1 - self.yl))
        if k and min(k + 2, 7) in ZC:
            for i, dx in enumerate((-1, 1, 2)):
                self.onward(k, "C%d" % (1 + i), dx)

    def ready(self):
        for cp in self.weights:
            cp.wait()
        self.weights = ()

    def A(self, k):
        self.ready()
        r = self.rows(k)
        t = self.tok[r, :]
        self.part[k, 0] = lax.dot_general(t, self.wg[...], NT, preferred_element_type=F32)
        self.part[k, 1] = lax.dot_general(t, self.wu[...], NT, preferred_element_type=F32)
        self.swap(k, 0, pl.ds(0, 2))

    def swap(self, k, i, arrays):
        other = pl.ds(pl.multiple_of((1 - self.c) * 64, 64), 64)
        self.send(("s1", k, i), self.part.at[k, arrays, other, :], self.s1.at[k, arrays], self.dev(c=1 - self.c))

    def F(self, k):
        r = self.rows(k)
        self.part[k, 2] = lax.dot_general(self.cot[r, :], self.wd[...], NT, preferred_element_type=F32)
        self.swap(k, 1, pl.ds(2, 1))

    def G(self, k):
        for i, arrays in ((0, pl.ds(0, 2)), (1, pl.ds(2, 1))):
            self.wait(("s1", k, i), self.s1.at[k, arrays], self.dev(c=1 - self.c))
        mine = pl.ds(pl.multiple_of(self.c * 64, 64), 64)
        rest = []
        for i in range(3):
            total = self.part[k, i, mine, :] + self.s1[k, i]
            self.s1[k, i] = total
            low = total.astype(BF)
            for t in range(3):
                self.g2[k, (i * 3 + t) * 64 : (i * 3 + t + 1) * 64, :] = low[:, t * 128 : (t + 1) * 128]
            rest.append(low[:, 384:])
        self.g2[k, 576:640, :] = jnp.concatenate(rest[:2], axis=1)
        self.g2[k, 640:, :] = jnp.concatenate([rest[2][:32], rest[2][32:]], axis=1)
        self.send(("s2", k), self.g2.at[k], self.s2.at[k], self.dev(yh=1 - self.yh))

    def H(self, k):
        self.wait(("s2", k), self.s2.at[k], self.dev(yh=1 - self.yh))
        r = self.side(k, self.c)
        pair, last = self.s2[k, 576:640, :], self.s2[k, 640:, :]
        rest = (pair[:, :64], pair[:, 64:], jnp.concatenate([last[:, :64], last[:, 64:]], axis=0))
        for t in range(4):
            cs = pl.ds(t * 128, 128 if t < 3 else 64)
            far = [self.s2[k, (i * 3 + t) * 64 : (i * 3 + t + 1) * 64, :] if t < 3 else rest[i] for i in range(3)]
            gate, up, grad = (self.s1[k, i, :, cs] + far[i].astype(F32) for i in range(3))
            s = jax.nn.sigmoid(gate)
            a = gate * s
            self.back[0, r, cs] = (a * up).astype(BF)
            self.back[1, r, cs] = (grad * up * (s * (1.0 + gate * (1.0 - s)))).astype(BF)
            self.back[2, r, cs] = (grad * a).astype(BF)
        b = self.back.at[:, r, :]
        self.send(("s4", k), b, b, self.dev(c=1 - self.c))

    def J(self, k):
        self.wait(("s4", k), self.back.at[:, self.side(k, 1 - self.c), :], self.dev(c=1 - self.c))
        r = self.rows(k)
        self.tot[k] = jnp.dot(self.back[1, r, :], self.wg[...], preferred_element_type=F32) + jnp.dot(
            self.back[2, r, :], self.wu[...], preferred_element_type=F32
        )
        if k in YF:
            i = YF.index(k)
            for b in range(NX):
                self.by4[i, b * SH : (b + 1) * SH] = self.tot[k, self.strip(b, 1 - self.yl), :].astype(BF)
            self.send(("ry", k), self.by4.at[i], self.ry4.at[i], self.dev(yl=1 - self.yl))
        else:
            self.over_x(k)

    def strip(self, b, y):
        return pl.ds(pl.multiple_of(b * PAIR + y * SH, SH), SH)

    def Y(self, k):
        i = YF.index(k)
        self.wait(("ry", k), self.ry4.at[i], self.dev(yl=1 - self.yl))
        for b in range(NX):
            r = self.strip(b, self.yl)
            self.tot[k, r, :] = self.tot[k, r, :] + self.ry4[i, b * SH : (b + 1) * SH].astype(F32)
        self.over_x(k)

    def block(self, k, dx):
        if k in YF:
            return self.strip(self.xblock(dx), self.yl)
        return pl.ds(pl.multiple_of(self.xblock(dx) * PAIR, PAIR), PAIR)

    def over_x(self, k):
        n = pl.ds(0, SH if k in YF else PAIR)
        self.b1[k, n] = self.tot[k, self.block(k, 2), :].astype(BF)
        if k in DIRECT:
            self.send(("r1", k), self.b1.at[k, n], self.r1.at[k, n], self.dev(dx=2))
            for q in (0, 1):
                self.b2[k, q, n] = self.tot[k, self.block(k, 1 if q == 0 else -1), :].astype(BF)
                self.send(("r2", k, q), self.b2.at[k, q, n], self.r2.at[k, q, n], self.xd(q))
        else:
            for q in (0, 1):
                self.send(("r1", k, q), self.b1.at[k, n, self.half[q]], self.r1.at[k, n, self.half[q]], self.xd(q))

    def K(self, k):
        n = pl.ds(0, SH if k in YF else PAIR)
        for q in (0, 1):
            h, o = self.half[q], self.half[1 - q]
            self.wait(("r1", k, q), self.r1.at[k, n, h], self.xd(1 - q))
            b = self.block(k, 1 if q == 0 else -1)
            self.b2[k, q, n, h] = (self.tot[k, b, h] + self.r1[k, n, h].astype(F32)).astype(BF)
            self.b2[k, q, n, o] = self.tot[k, b, o].astype(BF)
            self.send(("r2", k, q), self.b2.at[k, q, n], self.r2.at[k, q, n], self.xd(q))

    def L(self, k):
        n = pl.ds(0, SH if k in YF else PAIR)
        for q in (0, 1):
            self.wait(("r2", k, q), self.r2.at[k, q, n], self.xd(1 - q))
        b = self.block(k, 0)
        s = self.tot[k, b, :] + self.r2[k, 0, n].astype(F32) + self.r2[k, 1, n].astype(F32)
        if k in DIRECT:
            self.wait(("r1", k), self.r1.at[k, n], self.dev(dx=2))
            s = s + self.r1[k, n].astype(F32)
        if k in YF:
            self.over_z(k, s)
            return
        self.tot[k, b, :] = s
        if k in FAR:
            for i, y in ((0, self.yl), (1, 1 - self.yl)):
                self.bz[k, i] = self.tot[k, self.yrows(y), :].astype(BF)
                self.send(("rz", k, i), self.bz.at[k, i], self.rz.at[k, i], self.dev(dz=offset(k), yl=y))
        else:
            self.by[k] = self.tot[k, self.yrows(1 - self.yl), :].astype(BF)
            self.send(("ry", k), self.by.at[k], self.ry.at[k], self.dev(yl=1 - self.yl))

    def yrows(self, y):
        return self.strip(self.xblock(0), y)

    def over_z(self, k, s):
        if k == 0:
            self.tot[k, self.yrows(self.yl), :] = s
        else:
            self.bz[k, 0] = s.astype(BF)
            self.send(("rz", k, 0), self.bz.at[k, 0], self.rz.at[k, 0], self.dev(dz=offset(k)))

    def M(self, k):
        self.wait(("ry", k), self.ry.at[k], self.dev(yl=1 - self.yl))
        self.over_z(k, self.tot[k, self.yrows(self.yl), :] + self.ry[k].astype(F32))

    def N(self):
        s = self.tot[0, self.yrows(self.yl), :]
        for k in range(1, NZ):
            for i, y in ((0, self.yl), (1, 1 - self.yl))[: 2 if k in FAR and k not in YF else 1]:
                self.wait(("rz", k, i), self.rz.at[k, i], self.dev(dz=-offset(k), yl=y))
                s = s + self.rz[k, i].astype(F32)
        self.out[...] = s.astype(BF)

    def turn(self):
        for i in range(3):
            self.ht[i] = self.back[i].T

    def W(self, j):
        n = self.tok.shape[1] // TILES
        cs = pl.ds(j * n, n)
        for i, a, o in ((1, self.tok, self.og), (2, self.tok, self.ou), (0, self.cot, self.od)):
            o[:, cs] = jnp.dot(self.ht[i], a[:, cs], preferred_element_type=F32).astype(BF)

    def finish(self):
        self.ready()
        for cp in self.sent:
            cp.wait_send()


NAMES = {"z": "zin", "x": "xin", "ht": "turn"}


def kernel(*refs):
    step = Step(refs)
    step.begin()
    for name, *args in ORDER:
        getattr(step, NAMES.get(name, name))(*args)
    step.finish()


def hand_over(*refs):
    *arrays, sem = refs
    copies = [pltpu.make_async_copy(arrays[i], arrays[4 + i], sem.at[i]) for i in range(4)]
    for cp in copies:
        cp.start()
    for cp in copies:
        cp.wait()


def shards(tokens, grad_output, gate_weight, up_weight, down_weight):
    d, f = gate_weight.shape
    n = NZ * CHUNK
    anywhere = pl.BlockSpec(memory_space=pl.ANY)
    vmem = pltpu.VMEM
    results = pl.pallas_call(
        kernel,
        out_shape=(
            vmem((SH, d), BF),
            vmem((f, d), BF),
            vmem((f, d), BF),
            vmem((f, d), BF),
        ),
        in_specs=[anywhere] * 5,
        out_specs=(pl.BlockSpec(memory_space=vmem),) * 4,
        scratch_shapes=[
            vmem((n, d), BF), vmem((n, d), BF),
            vmem((f, d), BF), vmem((f, d), BF), vmem((f, d), BF),
            vmem((NZ, 3, CHUNK, f), F32), vmem((NZ, 3, 64, f), F32), vmem((NZ, 672, 128), BF), vmem((NZ, 672, 128), BF),
            vmem((3, n, f), BF),
            vmem((NZ, CHUNK, d), F32),
            vmem((NZ, PAIR, d), BF), vmem((NZ, 2, PAIR, d), BF),
            vmem((NZ, PAIR, d), BF), vmem((NZ, 2, PAIR, d), BF),
            vmem((NZ, SH, d), BF), vmem((NZ, SH, d), BF), vmem((NZ, 2, SH, d), BF), vmem((NZ, 2, SH, d), BF),
            vmem((max(1, len(YF)), NX * SH, d), BF), vmem((max(1, len(YF)), NX * SH, d), BF),
            vmem((3, f, n), BF),
            pltpu.SemaphoreType.DMA((200,)), pltpu.SemaphoreType.DMA((200,)), pltpu.SemaphoreType.DMA((5,)),
        ],
        compiler_params=pltpu.CompilerParams(collective_id=0, has_side_effects=True, vmem_limit_bytes=55 << 20),
        cost_estimate=pl.CostEstimate(flops=16 * n * d * f, bytes_accessed=12 * d * f, transcendentals=n * f),
    )(tokens, grad_output, gate_weight.T, up_weight.T, down_weight)
    grad_tokens, grad_gate, grad_up, grad_down = pl.pallas_call(
        hand_over,
        out_shape=tuple(jax.ShapeDtypeStruct(r.shape, r.dtype) for r in results),
        in_specs=[pl.BlockSpec(memory_space=vmem)] * 4,
        out_specs=(anywhere,) * 4,
        scratch_shapes=[pltpu.SemaphoreType.DMA((4,))],
        compiler_params=pltpu.CompilerParams(vmem_limit_bytes=1 << 20),
    )(*(pltpu.with_memory_space_constraint(r, vmem) for r in results))
    return grad_tokens, grad_gate.T, grad_up.T, grad_down


def solution(mesh):
    placed = (P("hid", "mod"), P("hid", "mod"), P("mod", "hid"), P("mod", "hid"), P("hid", "mod"))
    return jax.shard_map(
        shards,
        mesh=mesh,
        in_specs=placed,
        out_specs=(P("hid", "mod"), P("mod", "hid"), P("mod", "hid"), P("hid", "mod")),
        check_vma=False,
    )
```
